32 devices in a mesh: dp: 8 (over z, x), patch: 4 (over y, core).
Axes of the slice: x: 2, y: 2, z: 4, core: 2. Of those that a mesh axis runs over, the one named last changes fastest.
Arguments:
- images: bfloat16 [192, 324, 512], P('dp', 'patch'), may hold values from -6 to 6
- cotangent: bfloat16 [192, 324, 512], P('dp', 'patch'), may hold values from -6 to 6
- res_class: int32 [192], P('dp'), may hold values from 0 to 2
- skip: int32 [192], P('dp'), may hold values 0 or 1
- ln_gain: float32 [512], replicated, may hold values from 0.5 to 1.5
- ln_bias: float32 [512], replicated, may hold values from -3 to 3
- w_in: bfloat16 [512, 3072], replicated, may hold values from -0.25 to 0.25
- b_in: float32 [3072], replicated, may hold values from -3 to 3
- gate_gain: float32 [1536], replicated, may hold values from 0.5 to 1.5
- gate_bias: float32 [1536], replicated, may hold values from -3 to 3
- w_spatial: bfloat16 [324, 324], replicated, may hold values from -0.3125 to 0.3125
- b_spatial: float32 [324], replicated, may hold values from -4 to 4
- w_out: bfloat16 [1536, 512], replicated, may hold values from -0.15625 to 0.15625
- b_out: float32 [512], replicated, may hold values from -3 to 3
Outputs:
- output: bfloat16 [192, 324, 512], P('dp', 'patch')
- grad_images: float32 [192, 324, 512], P('dp', 'patch')
- grad_ln_gain: float32 [512], replicated
- grad_ln_bias: float32 [512], replicated
- grad_w_in: float32 [512, 3072], replicated
- grad_b_in: float32 [3072], replicated
- grad_gate_gain: float32 [1536], replicated
- grad_gate_bias: float32 [1536], replicated
- grad_w_spatial: float32 [324, 324], replicated
- grad_b_spatial: float32 [324], replicated
- grad_w_out: float32 [1536, 512], replicated
- grad_b_out: float32 [512], replicated
The draws below stay inside these ranges and needn't reach their ends.
All inputs are finite; a program needn't handle non-finite values. No bound on the sum of `skip` on one device may be relied on, other than what follows from the above.
Results may differ from the reference program's by a relative error of at most 0.0076.
Values may be sent and summed in bfloat16 or wider, within the bound.
A program may use at most 320 MiB of HBM per device.

```python
import jax
import jax.numpy as jnp
from jax import lax

D = 512
HID = 3072
HALF_W = 1536
SIDE_S = 10
SIDE_M = 14
SIDE_L = 18
PATCHES = 324
SLOT = 81
IMAGES = 192
N_PATCH = 4


def place_ends(values, own_key, low, largest):
    index_at = [jax.random.randint(jax.random.fold_in(own_key, axis), (), 0, length) for axis, length in enumerate(values.shape)]
    longest = values.shape.index(max(values.shape))
    neighbour = index_at[:longest] + [(index_at[longest] + 1) % values.shape[longest]] + index_at[longest + 1:]
    return values.at[tuple(index_at)].set(low).at[tuple(neighbour)].set(largest)


def block_levels(own_key, shape, split, smallest, high):
    def one(dim, shards_of):
        draws = jax.random.uniform(jax.random.fold_in(jax.random.fold_in(own_key, 6), dim), (shards_of,), jnp.float32, smallest / len(split), high / len(split))
        return jnp.repeat(jnp.exp(draws), shape[dim] // shards_of).reshape((-1,) + (1,) * (len(shape) - dim - 1))

    gain = one(*split[0])
    for cut in split[1:]:
        gain = gain * one(*cut)
    return gain


def scatter_about(own_key, shape, deviation, limit, cuts=(), held_as=jnp.bfloat16):
    factor_of = block_levels(own_key, shape, cuts, -0.22, 0.18) if cuts else 1.0
    values = jax.random.normal(own_key, shape, jnp.float32) * deviation * factor_of
    return jnp.minimum(jnp.maximum(values, -limit), limit).astype(held_as)


def setup_inputs(seed: int = 0) -> dict:
    key_list = jax.random.split(jax.random.key(seed), 15)
    images = scatter_about(key_list[0], (IMAGES, PATCHES, D), 1.0, 6.0, ((0, 8), (1, 4)))
    cotangent = scatter_about(key_list[1], (IMAGES, PATCHES, D), 1.0, 6.0, ((0, 8), (1, 4)))
    res_class = place_ends(jax.random.randint(key_list[2], (IMAGES,), 0, 3), jax.random.fold_in(key_list[2], 1), 0, 2).astype(jnp.int32)
    skip = place_ends((jax.random.randint(key_list[3], (IMAGES,), 0, 10) < 9).astype(jnp.int32), jax.random.fold_in(key_list[3], 1), 0, 1)
    ln_gain = jnp.clip(1.0 + 0.1 * jax.random.normal(key_list[4], (D,), jnp.float32), 0.5, 1.5)
    ln_bias = scatter_about(key_list[5], (D,), 0.5, 3.0, (), jnp.float32)
    w_in = scatter_about(key_list[6], (D, HID), D ** -0.5, 0.25)
    b_in = scatter_about(key_list[7], (HID,), 0.5, 3.0, (), jnp.float32)
    gate_gain = jnp.clip(1.0 + 0.1 * jax.random.normal(key_list[8], (HALF_W,), jnp.float32), 0.5, 1.5)
    gate_bias = scatter_about(key_list[9], (HALF_W,), 0.5, 3.0, (), jnp.float32)
    w_spatial = scatter_about(key_list[10], (PATCHES, PATCHES), PATCHES ** -0.5, 0.3125)
    b_spatial = scatter_about(key_list[11], (PATCHES,), 1.0, 4.0, (), jnp.float32)
    w_out = scatter_about(key_list[12], (HALF_W, D), HALF_W ** -0.5, 0.15625)
    b_out = scatter_about(key_list[13], (D,), 0.5, 3.0, (), jnp.float32)
    return {"images": images, "cotangent": cotangent, "res_class": res_class, "skip": skip, "ln_gain": ln_gain, "ln_bias": ln_bias, "w_in": w_in, "b_in": b_in, "gate_gain": gate_gain, "gate_bias": gate_bias, "w_spatial": w_spatial, "b_spatial": b_spatial, "w_out": w_out, "b_out": b_out}


@jax.custom_vjp
def low(v):
    return lax.optimization_barrier(v.astype(jnp.bfloat16)).astype(jnp.float32)

@jax.custom_vjp
def low_back(v):
    return v

def low_keep(v):
    return (low(v), None)

def low_pass(kept, grad):
    return (grad,)

def back_keep(v):
    return (v, None)

def back_low(kept, grad):
    return (low(grad),)
low.defvjp(low_keep, low_pass)
low_back.defvjp(back_keep, back_low)
epsilon = 1e-05

def slot_tables(slot_count, groups):
    total_slots = slot_count * groups
    slot_index = jnp.arange(total_slots, dtype=jnp.int32)
    block_of = slot_index // slot_count
    within = slot_index % slot_count
    target = jnp.arange(total_slots, dtype=jnp.int32)
    tables = []
    live_rows = []
    for side_len in (SIDE_S, SIDE_M, SIDE_L):
        per_group = side_len * side_len // groups
        is_live = within < per_group
        where_to = block_of * per_group + within
        tables.append((is_live[:, None] & (where_to[:, None] == target[None, :])).astype(jnp.float32))
        live_rows.append(is_live.astype(jnp.float32))
    return (jnp.stack(tables), jnp.stack(live_rows))

def layer_norm(values, gain_vec, shift_vec):
    centred = values - lax.optimization_barrier(jnp.mean(values, axis=-1, keepdims=True))
    inv_std = lax.rsqrt(lax.optimization_barrier(jnp.mean(centred * centred, axis=-1, keepdims=True)) + epsilon)
    return centred * inv_std * gain_vec + shift_vec

def image_block(params, inputs, one_hot, skip_scale, select, live_rows):
    highest = lax.Precision.HIGHEST
    ln_gain, ln_bias, w_in, b_in, gate_gain, gate_bias, w_spatial, b_spatial, w_out, b_out = params
    keep_scale = skip_scale[:, None] * jnp.einsum('ic,ct->it', one_hot, live_rows, precision=highest)
    act = low(layer_norm(inputs, ln_gain, ln_bias))
    z_pre = low_back(jnp.einsum('ird,df->irf', act, w_in, precision=highest) + b_in)
    z_act = jax.nn.gelu(z_pre)
    half_width = w_out.shape[0]
    u_half = z_act[..., :half_width]
    v_half = z_act[..., half_width:]
    gate = low(layer_norm(v_half, gate_gain, gate_bias))
    picked = jnp.einsum('cta,ab->ctb', select, w_spatial, precision=highest)
    rows_class = jnp.einsum('ctb,csb->cts', picked, select, precision=highest)
    rows_image = jnp.einsum('ic,cts->its', one_hot, rows_class, precision=highest)
    bias_class = jnp.einsum('cta,a->ct', select, b_spatial, precision=highest)
    bias_image = jnp.einsum('ic,ct->it', one_hot, bias_class, precision=highest)
    spatial = low_back(jnp.einsum('its,isc->itc', rows_image, gate, precision=highest) + bias_image[..., None])
    gated = low(u_half * spatial)
    branch = low_back(jnp.einsum('itc,cd->itd', gated, w_out, precision=highest) + b_out)
    return inputs + keep_scale[..., None] * branch

def reference(images, cotangent, res_class, skip, ln_gain, ln_bias, w_in, b_in, gate_gain, gate_bias, w_spatial, b_spatial, w_out, b_out):
    select, live_rows = slot_tables(SLOT, N_PATCH)
    one_hot = (res_class[:, None] == jnp.arange(3, dtype=jnp.int32)[None, :]).astype(jnp.float32)
    skip_scale = skip.astype(jnp.float32) / 0.9
    params = (ln_gain.astype(jnp.float32), ln_bias.astype(jnp.float32), w_in.astype(jnp.float32), b_in.astype(jnp.float32), gate_gain.astype(jnp.float32), gate_bias.astype(jnp.float32), w_spatial.astype(jnp.float32), b_spatial.astype(jnp.float32), w_out.astype(jnp.float32), b_out.astype(jnp.float32))
    inputs = images.astype(jnp.float32)
    width = inputs.shape[2]

    def forward(weights, values):
        blocked = values.reshape(-1, 4, PATCHES, width)
        hot_blocks = one_hot.reshape(-1, 4, 3)
        skip_blocks = skip_scale.reshape(-1, 4)
        checked = jax.checkpoint(image_block)

        def one_block(block_items):
            return checked(weights, block_items[0], block_items[1], block_items[2], select, live_rows)
        results = lax.map(one_block, (blocked, hot_blocks, skip_blocks))
        return results.reshape(values.shape)
    result, pull_back = jax.vjp(forward, params, inputs)
    grad_params, grad_inputs = pull_back(cotangent.astype(jnp.float32))
    return (result.astype(jnp.bfloat16), grad_inputs, grad_params[0], grad_params[1], grad_params[2], grad_params[3], grad_params[4], grad_params[5], grad_params[6], grad_params[7], grad_params[8], grad_params[9])
```

```python
import functools

import jax
import jax.numpy as jnp
import numpy as np
from jax import lax
from jax.experimental import pallas as pl
from jax.experimental.pallas import tpu as pltpu
from jax.sharding import PartitionSpec as P

MESH = pl.DeviceIdType.MESH
SIDES = (10, 14, 18)
EPS = 1e-05
F32 = jnp.float32
BF16 = jnp.bfloat16
CT = 256
KEEP = np.float32(1.0) / np.float32(0.9)
GELU_C = np.float32(np.sqrt(2.0 / np.pi))
GELU_K = np.float32(0.044715)


def up(value, unit):
    return -(-value // unit) * unit


def dot(a, b):
    return lax.dot_general(a, b, (((1,), (0,)), ((), ())), preferred_element_type=F32)


def dot_nt(a, b):
    return lax.dot_general(a, b, (((1,), (1,)), ((), ())), preferred_element_type=F32)


def dot_tn(a, b):
    return lax.dot_general(a, b, (((0,), (0,)), ((), ())), preferred_element_type=F32)


def gelu_both(z):
    z2 = z * z
    t = jnp.tanh(z * (GELU_C + (GELU_C * GELU_K) * z2))
    a = 0.5 + 0.5 * t
    g = z * a
    slope = a + (g * (1.0 - t)) * (GELU_C + (3.0 * GELU_C * GELU_K) * z2)
    return g, slope


def fold(v):
    total = v[:, :128]
    for i in range(1, v.shape[1] // 128):
        total = total + v[:, i * 128 : (i + 1) * 128]
    return total


def col8(v):
    return jnp.sum(v.reshape(v.shape[0] // 8, 8, v.shape[1]), axis=0)


def position(j, device, groups):
    return jnp.where(lax.rem(j, 2) == 0, device, groups - 1 - device)


def pack_kernel(slot_count, groups, me_ref, order_ref, img_ref, cot_ref, *refs):
    outs, stage = refs[:groups], refs[groups]
    j = pl.program_id(0)
    me = me_ref[0]
    for k in range(groups):
        which = order_ref[j * groups + position(j, me ^ k, groups)]
        stage[0:slot_count, :] = img_ref[which].astype(F32)
        stage[slot_count : 2 * slot_count, :] = cot_ref[which].astype(F32)
        outs[k][0] = stage[...].astype(BF16)


def unpack_kernel(slot_count, groups, quarter, me_ref, rank_ref, key_ref, img_ref, cot_ref, *refs):
    backs, out_ref, grad_ref, stage = refs[:groups], refs[groups], refs[groups + 1], refs[groups + 2]
    i = pl.program_id(0)
    me = me_ref[0]
    key = key_ref[i]
    slot = rank_ref[i] // groups
    place = lax.rem(rank_ref[i], groups)
    owner = position(slot, place, groups)
    x = img_ref[0].astype(F32)
    dy = cot_ref[0].astype(F32)
    out_ref[0] = img_ref[0]
    grad_ref[0] = dy
    for k in range(groups):

        @pl.when((key > 0) & ((me ^ owner) == k))
        def _(k=k):
            stage[...] = backs[k][slot].astype(F32)
            live = jnp.where(key == 3, quarter[2], jnp.where(key == 2, quarter[1], quarter[0]))
            row = lax.broadcasted_iota(jnp.int32, (slot_count, 1), 0)
            mask = row < live
            out_ref[0] = (x + jnp.where(mask, stage[0:slot_count, :], 0.0)).astype(BF16)
            grad_ref[0] = dy + jnp.where(mask, stage[slot_count : 2 * slot_count, :], 0.0)


def image_work(q, slot_count, me, ins, outs, par, acc, scr):
    groups = len(ins)
    n = groups * q
    rows = up(n, 16)
    width = scr["xs"].shape[1]
    half = scr["gate"].shape[1]
    tiles = half // CT
    xs, dys, stage, act, dbr = scr["xs"], scr["dys"], scr["stage"], scr["act"], scr["dbr"]
    vs, gvp, gate, gated, dsp, dgs, dpre = (
        scr["vs"], scr["gvp"], scr["gate"], scr["gated"], scr["dsp"], scr["dgs"], scr["dpre"],
    )
    if rows > n:
        xs[rows - 16 : rows, :] = jnp.zeros((16, width), F32)
        dys[rows - 16 : rows, :] = jnp.zeros((16, width), F32)
    for m in range(groups):

        @pl.when(me == m)
        def _(m=m):
            for k in range(groups):
                at = (m ^ k) * q
                stage[...] = ins[k][0].astype(F32)
                xs[at : at + q, :] = stage[0:q, :]
                dys[at : at + q, :] = stage[slot_count : slot_count + q, :]

    x = xs[0:rows, :]
    mean = jnp.mean(x, axis=-1, keepdims=True)
    cen = x - mean
    inv = lax.rsqrt(jnp.mean(cen * cen, axis=-1, keepdims=True) + EPS)
    xhat = cen * inv
    xs[0:rows, :] = xhat
    scr["inv"][0:rows, :] = jnp.broadcast_to(inv, (rows, 128))
    act[0:rows, :] = (xhat * par["ln_gain"][...] + par["ln_bias"][...]).astype(BF16)
    db = (dys[0:rows, :] * KEEP).astype(BF16)
    dbr[0:rows, :] = db
    acc["b_out"][...] += col8(db.astype(F32))

    @pl.loop(0, tiles)
    def _(t):
        at = pl.ds(pl.multiple_of(t * CT, CT), CT)
        far = pl.ds(pl.multiple_of(half + t * CT, CT), CT)
        z = dot(act[0:rows, :], par["w_in"][:, far]) + par["b_in"][:, far]
        g, slope = gelu_both(z)
        vs[0:rows, at] = g
        gvp[0:rows, at] = slope.astype(BF16)

    total = fold(vs[0:rows, :])
    vmean = jnp.sum(total, axis=-1, keepdims=True) / half
    cen = vs[0:rows, :] - vmean
    vinv = lax.rsqrt(jnp.sum(fold(cen * cen), axis=-1, keepdims=True) / half + EPS)
    vhat = cen * vinv
    vs[0:rows, :] = vhat
    gate[0:rows, :] = (vhat * par["gate_gain"][...] + par["gate_bias"][...]).astype(BF16)
    if rows > n:
        tail = lax.broadcasted_iota(jnp.int32, (16, 1), 0) < n - (rows - 16)
        gate[rows - 16 : rows, :] = jnp.where(tail, gate[rows - 16 : rows, :].astype(F32), 0.0).astype(BF16)
    scr["hs"][0:rows, :] = jnp.zeros((rows, 128), F32)
    scr["hv"][0:rows, :] = jnp.zeros((rows, 128), F32)
    c = SIDES.index(int(round(np.sqrt(n))))

    @pl.loop(0, tiles)
    def _(t):
        at = pl.ds(pl.multiple_of(t * CT, CT), CT)
        z = dot(act[0:rows, :], par["w_in"][:, at]) + par["b_in"][:, at]
        u, slope = gelu_both(z)
        sp = dot(par["wsp"][c, 0:rows, 0:rows], gate[0:rows, at]) + par["bsp"][c, 0:rows, 0:1]
        gated[0:rows, at] = (u * sp).astype(BF16)
        dg = dot(dbr[0:rows, :], par["w_out_t"][:, at])
        pre = (dg * sp * slope).astype(BF16)
        dpre[0:rows, at] = pre
        acc["b_in"][:, at] += col8(pre.astype(F32))
        ds = (dg * u).astype(BF16)
        dsp[0:rows, at] = ds
        acc["b_sp"][0:rows, :] += fold(ds.astype(F32))
        dgate = dot(par["wsp_t"][c, 0:rows, 0:rows], ds)
        vh = vs[0:rows, at]
        acc["gate_bias"][:, at] += col8(dgate)
        acc["gate_gain"][:, at] += col8(dgate * vh)
        h = dgate * par["gate_gain"][:, at]
        dgs[0:rows, at] = h
        scr["hs"][0:rows, :] += fold(h)
        scr["hv"][0:rows, :] += fold(h * vh)

    hmean = jnp.sum(scr["hs"][0:rows, :], axis=-1, keepdims=True) / half
    hvmean = jnp.sum(scr["hv"][0:rows, :], axis=-1, keepdims=True) / half

    @pl.loop(0, tiles)
    def _(t):
        at = pl.ds(pl.multiple_of(t * CT, CT), CT)
        far = pl.ds(pl.multiple_of(half + t * CT, CT), CT)
        dv = vinv * (dgs[0:rows, at] - hmean - vs[0:rows, at] * hvmean)
        pre = (dv * gvp[0:rows, at].astype(F32)).astype(BF16)
        dpre[0:rows, far] = pre
        acc["b_in"][:, far] += col8(pre.astype(F32))

    acc["w_sp"][0:rows, 0:rows] += dot_nt(dsp[0:rows, :], gate[0:rows, :])
    branch = dot(gated[0:rows, :], par["w_out"][...]) + par["b_out"][...]
    dys[0:rows, :] = branch * KEEP
    dact = dot(dpre[0:rows, :], par["w_in_t"][...])
    xhat = xs[0:rows, :]
    acc["ln_bias"][...] += col8(dact)
    acc["ln_gain"][...] += col8(dact * xhat)
    h = dact * par["ln_gain"][...]
    back = scr["inv"][0:rows, 0:1] * (
        h - jnp.mean(h, axis=-1, keepdims=True) - xhat * jnp.mean(h * xhat, axis=-1, keepdims=True)
    )
    xs[0:rows, :] = back
    for m in range(groups):

        @pl.when(me == m)
        def _(m=m):
            for k in range(groups):
                at = (m ^ k) * q
                stage[0:q, :] = dys[at : at + q, :]
                stage[slot_count : slot_count + q, :] = xs[at : at + q, :]
                outs[k][0] = stage[...].astype(BF16)

    act_t = act[0:rows, :].T
    dbr_t = dbr[0:rows, :].T

    @pl.loop(0, 2 * tiles)
    def _(t):
        at = pl.ds(pl.multiple_of(t * CT, CT), CT)
        acc["w_in"][:, at] += dot(act_t, dpre[0:rows, at])

    @pl.loop(0, tiles)
    def _(t):
        at = pl.ds(pl.multiple_of(t * CT, CT), CT)
        acc["w_out_t"][:, at] += dot(dbr_t, gated[0:rows, at])


PAR = ("ln_gain", "ln_bias", "w_in", "w_in_t", "b_in", "gate_gain", "gate_bias", "wsp", "wsp_t", "bsp", "w_out", "w_out_t", "b_out")
ACC = ("w_in", "w_out_t", "w_sp", "b_in", "gate_gain", "gate_bias", "ln_gain", "ln_bias", "b_out", "b_sp")
SCR = ("stage", "xs", "dys", "inv", "act", "dbr", "vs", "gvp", "gate", "gated", "dsp", "dgs", "dpre", "hs", "hv")


def compute_kernel(slot_count, groups, quarter, me_ref, cls_ref, *refs):
    ins, refs = refs[:groups], refs[groups:]
    par, refs = dict(zip(PAR, refs)), refs[len(PAR) :]
    outs, refs = refs[:groups], refs[groups:]
    total_ref, refs = refs[0], refs[1:]
    acc, refs = dict(zip(ACC, refs)), refs[len(ACC) :]
    scr = dict(zip(SCR, refs))
    j = pl.program_id(0)
    me = me_ref[0]

    @pl.when(j == 0)
    def _():
        for ref in acc.values():
            ref[...] = jnp.zeros_like(ref)

    for c, q in enumerate(quarter):

        @pl.when(cls_ref[j] == c + 1)
        def _(q=q):
            image_work(q, slot_count, me, ins, outs, par, acc, scr)

    @pl.when(j == pl.num_programs(0) - 1)
    def _():
        width, wide = acc["w_in"].shape
        half = acc["w_out_t"].shape[1]
        total_ref[:, 0:wide] = acc["w_in"][...].astype(BF16)
        total_ref[:, wide : wide + half] = acc["w_out_t"][...].astype(BF16)
        base = wide + half
        side = acc["w_sp"].shape[0]
        total_ref[:, base:] = jnp.zeros((width, total_ref.shape[1] - base), BF16)
        span = acc["w_sp"].shape[1]
        total_ref[0:side, base : base + span] = acc["w_sp"][...].astype(BF16)
        sums = jnp.sum(acc["b_sp"][...], axis=-1, keepdims=True)
        total_ref[0:side, base + span : base + span + 128] = jnp.broadcast_to(sums, (side, 128)).astype(BF16)

        def line(name):
            return jnp.sum(acc[name][...], axis=0, keepdims=True)

        lines = []
        for name in ("b_in", "gate_gain", "gate_bias", "ln_gain", "ln_bias", "b_out"):
            v = line(name)
            lines += [v[:, i * width : (i + 1) * width] for i in range(v.shape[1] // width)]
        lines.append(jnp.zeros((16 - len(lines), width), F32))
        total_ref[side : side + 16, base : base + width] = jnp.concatenate(lines, axis=0).astype(BF16)


def reduce_plan(dp, patch, rows):
    dp_bits = [("dp", 1 << b) for b in range(dp.bit_length() - 1)]
    orders = [dp_bits[:1] + [("patch", 2)] + dp_bits[1:], [("patch", 2)] + dp_bits]
    plans = []
    for order in orders:
        size, steps = rows, []
        for axis, bit in order:
            halves = size // 2 >= 16
            steps.append((axis, bit, size, halves))
            size = size // 2 if halves else size
        plans.append(steps)
    return plans


def reduce_kernel(plans, pieces, g_ref, out_ref, acc, first, *refs):
    depth = len(plans[0])
    rbufs, (send_sem, recv_sem) = refs[:depth], refs[depth:]
    dp, patch = lax.axis_index("dp"), lax.axis_index("patch")
    core = patch & 1

    def peer(axis, bit):
        return (dp ^ bit, patch) if axis == "dp" else (dp, patch ^ bit)

    peers = [peer("patch", 1)] + [peer(a, b) for a, b, _, _ in plans[0]]
    barrier = pltpu.get_barrier_semaphore()
    for other in peers:
        pl.semaphore_signal(barrier, inc=1, device_id=other, device_id_type=MESH)
    pl.semaphore_wait(barrier, len(peers))

    rows, half = acc.shape
    cut = half // pieces
    mine = pl.multiple_of(core * half, 128)
    theirs = pl.multiple_of((1 - core) * half, 128)
    copies = []

    def send(src, dst, step, i, other):
        copy = pltpu.make_async_remote_copy(
            src_ref=src, dst_ref=dst, send_sem=send_sem.at[step, i], recv_sem=recv_sem.at[step, i],
            device_id=other, device_id_type=MESH,
        )
        copy.start()
        copies.append(copy)
        return copy

    def cols(i):
        return pl.ds(i * cut, cut)

    def shifted(base, i):
        return pl.ds(pl.multiple_of(base + i * cut, 128), cut)

    state = []
    flying = [
        send(g_ref.at[:, shifted(theirs, i)], first.at[:, cols(i)], 0, i, peer("patch", 1)) for i in range(pieces)
    ]
    for s in range(depth + 1):
        for i in range(pieces):
            plan = plans[i % 2]
            flying[i].wait_recv()
            if s == 0:
                lo = 0

                @pl.loop(0, rows, step=32)
                def _(r, i=i):
                    at = pl.ds(pl.multiple_of(r, 32), 32)
                    acc[at, cols(i)] = (
                        g_ref[at, shifted(mine, i)].astype(F32) + first[at, cols(i)].astype(F32)
                    ).astype(BF16)

                state.append(lo)
            else:
                axis, bit, size, halves = plan[s - 1]
                keep = size // 2 if halves else size
                lo = state[i]
                if not halves:
                    flying[i].wait_send()
                    copies[:] = [copy for copy in copies if copy is not flying[i]]
                unit = 16

                @pl.loop(0, keep, step=unit)
                def _(r, i=i, lo=lo, s=s):
                    at = pl.ds(pl.multiple_of(lo + r, unit), unit)
                    got = pl.ds(pl.multiple_of(r, unit), unit)
                    acc[at, cols(i)] = (
                        acc[at, cols(i)].astype(F32) + rbufs[s - 1][got, cols(i)].astype(F32)
                    ).astype(BF16)

            if s < depth:
                axis, bit, size, halves = plan[s]
                index = dp if axis == "dp" else patch
                up_half = jnp.where((index & bit) != 0, 1, 0)
                if halves:
                    keep = size // 2
                    give = pl.multiple_of(state[i] + (1 - up_half) * keep, 16)
                    state[i] = pl.multiple_of(state[i] + up_half * keep, 16)
                else:
                    keep, give = size, state[i]
                flying[i] = send(
                    acc.at[pl.ds(give, keep), cols(i)], rbufs[s].at[pl.ds(0, keep), cols(i)], s + 1, i, peer(axis, bit)
                )
    for i in range(pieces):
        axis, bit, size, halves = plans[i % 2][-1]
        keep = size // 2 if halves else size
        at = pl.ds(pl.multiple_of(state[i], 16), keep)
        out_ref[at, shifted(mine, i)] = acc[at, cols(i)]
    flying = [None] * pieces
    for s in range(depth, -1, -1):
        for i in range(pieces):
            if flying[i] is not None:
                flying[i].wait_recv()
                flying[i] = None
            step = 2 * depth + 1 - s
            if s == 0:
                at = pl.ds(0, rows)
                where = out_ref.at[at, shifted(mine, i)]
                flying[i] = send(where, where, step, i, peer("patch", 1))
            else:
                axis, bit, size, halves = plans[i % 2][s - 1]
                if not halves:
                    continue
                keep = size // 2
                index = dp if axis == "dp" else patch
                up_half = jnp.where((index & bit) != 0, 1, 0)
                where = out_ref.at[pl.ds(pl.multiple_of(state[i], 16), keep), shifted(mine, i)]
                flying[i] = send(where, where, step, i, peer(axis, bit))
                state[i] = state[i] - up_half * keep
    for i in range(pieces):
        flying[i].wait_recv()
    for copy in copies:
        copy.wait_send()


def all_reduce(total, dp, patch):
    rows, columns = total.shape
    plans = reduce_plan(dp, patch, rows)
    depth, half, pieces = len(plans[0]), columns // 2, 4
    sizes = [size // 2 if halves else size for _, _, size, halves in plans[0]]
    vmem = pl.BlockSpec(memory_space=pltpu.VMEM)
    return pl.pallas_call(
        functools.partial(reduce_kernel, plans, pieces),
        out_shape=jax.ShapeDtypeStruct(total.shape, total.dtype),
        in_specs=[vmem],
        out_specs=vmem,
        scratch_shapes=[pltpu.VMEM((rows, half), BF16), pltpu.VMEM((rows, half), BF16)]
        + [pltpu.VMEM((size, half), BF16) for size in sizes]
        + [pltpu.SemaphoreType.DMA((2 * depth + 2, pieces))] * 2,
        compiler_params=pltpu.CompilerParams(
            collective_id=1, has_side_effects=True, vmem_limit_bytes=40 * 1024 * 1024
        ),
        name="sum_gradients",
    )(total)


def local(images, cotangent, res_class, skip, ln_gain, ln_bias, w_in, b_in, gate_gain, gate_bias, w_spatial, b_spatial, w_out, b_out):
    groups = lax.axis_size("patch")
    dp = lax.axis_size("dp")
    count, slot_count, width = images.shape
    half = w_out.shape[0]
    wide = w_in.shape[1]
    slots = count // groups
    quarter = tuple(side * side // groups for side in SIDES)
    patches = groups * slot_count
    side = up(patches, 16)
    span = up(patches, 128)
    stage_rows = up(2 * slot_count, 16)
    me = lax.axis_index("patch").astype(jnp.int32)

    key = jnp.where(skip != 0, res_class + 1, 0).astype(jnp.int32)
    index = jnp.arange(count, dtype=jnp.int32)
    before = (key[None, :] > key[:, None]) | ((key[None, :] == key[:, None]) & (index[None, :] < index[:, None]))
    rank = jnp.sum(before.astype(jnp.int32), axis=1)
    hit = rank[None, :] == index[:, None]
    order = jnp.sum(jnp.where(hit, index[None, :], 0), axis=1)
    sorted_key = jnp.sum(jnp.where(hit, key[None, :], 0), axis=1)
    slot_index = jnp.arange(slots, dtype=jnp.int32)
    spot = slot_index * groups + jnp.where(slot_index % 2 == 0, me, groups - 1 - me)
    cls = jnp.sum(jnp.where(spot[:, None] == index[None, :], sorted_key[None, :], 0), axis=1)
    me1 = me.reshape(1)

    whole = pl.BlockSpec(memory_space=pltpu.VMEM)
    block = pl.BlockSpec((1, stage_rows, width), lambda j, *_: (j, 0, 0))
    parcel = jax.ShapeDtypeStruct((slots, stage_rows, width), BF16)
    packed = pl.pallas_call(
        functools.partial(pack_kernel, slot_count, groups),
        out_shape=[parcel] * groups,
        grid_spec=pltpu.PrefetchScalarGridSpec(
            num_scalar_prefetch=2, grid=(slots,), in_specs=[whole, whole], out_specs=[block] * groups,
            scratch_shapes=[pltpu.VMEM((stage_rows, width), F32)],
        ),
        name="pack",
    )(me1, order, images, cotangent)

    def swap(parts):
        return [parts[0]] + [
            lax.ppermute(parts[k], "patch", [(i, i ^ k) for i in range(groups)]) for k in range(1, groups)
        ]

    arrived = swap(packed)

    row = jnp.arange(side, dtype=jnp.int32)
    w_pad = jnp.pad(w_spatial, ((0, side - patches), (0, side - patches)))
    b_pad = jnp.pad(b_spatial, (0, side - patches))
    masks = [(row < groups * q) for q in quarter]
    wsp = jnp.stack([jnp.where(m[:, None] & m[None, :], w_pad, 0) for m in masks]).astype(BF16)
    wsp_t = jnp.swapaxes(wsp, 1, 2)
    bsp = jnp.stack([jnp.broadcast_to(jnp.where(m, b_pad, 0.0)[:, None], (side, 128)) for m in masks])
    par = {
        "ln_gain": ln_gain[None, :], "ln_bias": ln_bias[None, :], "w_in": w_in, "w_in_t": w_in.T, "b_in": b_in[None, :],
        "gate_gain": gate_gain[None, :], "gate_bias": gate_bias[None, :], "wsp": wsp, "wsp_t": wsp_t, "bsp": bsp,
        "w_out": w_out, "w_out_t": w_out.T, "b_out": b_out[None, :],
    }
    acc = {
        "w_in": (width, wide), "w_out_t": (width, half), "w_sp": (side, span), "b_in": (8, wide), "gate_gain": (8, half),
        "gate_bias": (8, half), "ln_gain": (8, width), "ln_bias": (8, width), "b_out": (8, width), "b_sp": (side, 128),
    }
    scr = {
        "stage": ((stage_rows, width), F32), "xs": ((side, width), F32), "dys": ((side, width), F32),
        "inv": ((side, 128), F32), "act": ((side, width), BF16), "dbr": ((side, width), BF16), "vs": ((side, half), F32),
        "gvp": ((side, half), BF16), "gate": ((side, half), BF16), "gated": ((side, half), BF16), "dsp": ((side, half), BF16),
        "dgs": ((side, half), F32), "dpre": ((side, wide), BF16), "hs": ((side, 128), F32), "hv": ((side, 128), F32),
    }
    columns = wide + half + 512
    results = pl.pallas_call(
        functools.partial(compute_kernel, slot_count, groups, quarter),
        out_shape=[parcel] * groups + [jax.ShapeDtypeStruct((width, columns), BF16)],
        grid_spec=pltpu.PrefetchScalarGridSpec(
            num_scalar_prefetch=2, grid=(slots,), in_specs=[block] * groups + [whole] * len(PAR),
            out_specs=[block] * groups + [whole],
            scratch_shapes=[pltpu.VMEM(acc[name], F32) for name in ACC] + [pltpu.VMEM(*scr[name]) for name in SCR],
        ),
        compiler_params=pltpu.CompilerParams(vmem_limit_bytes=60 * 1024 * 1024),
        name="images",
    )(me1, cls, *arrived, *[par[name] for name in PAR])
    returned = swap(results[:groups])
    summed = all_reduce(results[groups], dp, groups)

    own = pl.BlockSpec((1, slot_count, width), lambda i, *_: (i, 0, 0))
    output, grad_images = pl.pallas_call(
        functools.partial(unpack_kernel, slot_count, groups, quarter),
        out_shape=[jax.ShapeDtypeStruct(images.shape, BF16), jax.ShapeDtypeStruct(images.shape, F32)],
        grid_spec=pltpu.PrefetchScalarGridSpec(
            num_scalar_prefetch=3, grid=(count,), in_specs=[own, own] + [whole] * groups, out_specs=[own, own],
            scratch_shapes=[pltpu.VMEM((stage_rows, width), F32)],
        ),
        name="unpack",
    )(me1, rank, key, images, cotangent, *returned)

    base = wide + half
    small = summed[:, base:].astype(F32)
    lines = small[side : side + 16].reshape(-1)
    ends = np.cumsum([0, wide, half, half, width, width, width])
    g_b_in, g_gate_gain, g_gate_bias, g_ln_gain, g_ln_bias, g_b_out = [
        lines[ends[i] : ends[i + 1]] for i in range(6)
    ]
    return (
        output, grad_images, g_ln_gain, g_ln_bias, summed[:, :wide].astype(F32), g_b_in, g_gate_gain, g_gate_bias,
        small[:patches, :patches], small[:patches, span], summed[:, wide:base].T.astype(F32), g_b_out,
    )


def solution(mesh):
    placed = (P("dp", "patch", None),) * 2 + (P("dp"),) * 2 + (P(),) * 10
    return jax.shard_map(
        local, mesh=mesh, in_specs=placed, out_specs=(P("dp", "patch", None),) * 2 + (P(),) * 10, check_vma=False,
    )
```

```python
import functools

import jax
import jax.numpy as jnp
import numpy as np
from jax import lax
from jax.experimental import pallas as pl
from jax.experimental.pallas import tpu as pltpu
from jax.sharding import PartitionSpec as P

MESH = pl.DeviceIdType.MESH
SIDES = (10, 14, 18)
EPS = 1e-05
F32 = jnp.float32
BF16 = jnp.bfloat16
CT = 256
EARLY = 2
PIECES = (("c", 1), ("d", 2), ("b", 2)) * 4
KEEP = np.float32(1.0) / np.float32(0.9)
GELU_C = np.float32(np.sqrt(2.0 / np.pi))
GELU_K = np.float32(0.044715)


def up(value, unit):
    return -(-value // unit) * unit


def dot(a, b):
    return lax.dot_general(a, b, (((1,), (0,)), ((), ())), preferred_element_type=F32)


def dot_nt(a, b):
    return lax.dot_general(a, b, (((1,), (1,)), ((), ())), preferred_element_type=F32)


def dot_tn(a, b):
    return lax.dot_general(a, b, (((0,), (0,)), ((), ())), preferred_element_type=F32)


def gelu_both(z):
    z2 = z * z
    t = jnp.tanh(z * (GELU_C + (GELU_C * GELU_K) * z2))
    a = 0.5 + 0.5 * t
    g = z * a
    slope = a + (g * (1.0 - t)) * (GELU_C + (3.0 * GELU_C * GELU_K) * z2)
    return g, slope


def fold(v):
    total = v[:, :128]
    for i in range(1, v.shape[1] // 128):
        total = total + v[:, i * 128 : (i + 1) * 128]
    return total


def col8(v):
    return jnp.sum(v.reshape(v.shape[0] // 8, 8, v.shape[1]), axis=0)


def pack_kernel(slot_count, groups, me_ref, order_ref, img_ref, cot_ref, *refs):
    outs, (xf, yf, stage) = refs[:-3], refs[-3:]
    me = me_ref[0]
    count = img_ref.shape[1]
    lanes = xf.shape[0]

    @pl.loop(0, slot_count, unroll=9)
    def _(r):
        at = pl.ds(pl.multiple_of(r * count, 8), count)
        for c in range(lanes):
            xf[c, at, :] = img_ref[r, :, c * 128 : (c + 1) * 128].astype(F32)
            yf[c, at, :] = cot_ref[r, :, c * 128 : (c + 1) * 128].astype(F32)

    for j in range(outs[0].shape[0]):
        for k in range(groups):
            dest = me ^ k
            which = order_ref[j * groups + (dest if j % 2 == 0 else groups - 1 - dest)]
            for c in range(lanes):
                cols = slice(c * 128, (c + 1) * 128)
                stage[0:slot_count, cols] = xf[c, pl.ds(which, slot_count, stride=count), :]
                stage[slot_count : 2 * slot_count, cols] = yf[c, pl.ds(which, slot_count, stride=count), :]
            outs[k][j] = stage[...].astype(BF16)


def unpack_kernel(slot_count, quarter, rank_ref, key_ref, img_ref, cot_ref, back_ref, out_ref, grad_ref, xf, yf, stage):
    lanes = xf.shape[0]
    count = img_ref.shape[1]

    @pl.loop(0, slot_count, unroll=9)
    def _(r):
        at = pl.ds(pl.multiple_of(r * count, 8), count)
        for c in range(lanes):
            xf[c, at, :] = img_ref[r, :, c * 128 : (c + 1) * 128].astype(F32)
            yf[c, at, :] = cot_ref[r, :, c * 128 : (c + 1) * 128].astype(F32)

    @pl.loop(0, count)
    def _(i):
        key = key_ref[i]
        for c, q in enumerate(quarter):

            @pl.when(key == c + 1)
            def _(q=q):
                stage[...] = back_ref[rank_ref[i]].astype(F32)
                at = pl.ds(i, q, stride=count)
                for b in range(lanes):
                    cols = slice(b * 128, (b + 1) * 128)
                    xf[b, at, :] = xf[b, at, :] + stage[0:q, cols]
                    yf[b, at, :] = yf[b, at, :] + stage[slot_count : slot_count + q, cols]

    @pl.loop(0, slot_count, unroll=9)
    def _(r):
        at = pl.ds(pl.multiple_of(r * count, 8), count)
        for c in range(lanes):
            out_ref[r, :, c * 128 : (c + 1) * 128] = xf[c, at, :].astype(BF16)
            grad_ref[r, :, c * 128 : (c + 1) * 128] = yf[c, at, :]


def widen_kernel(first, src_ref, in_ref, out_ref):
    t = pl.program_id(0)

    @pl.when(t < first)
    def _():
        in_ref[...] = src_ref[...].astype(F32)

    @pl.when(t >= first)
    def _():
        out_ref[...] = src_ref[...].astype(F32).T


def image_work(kind, slot, slot_count, me, parcel, par, acc, scr):
    groups = parcel.shape[0]
    rows = scr["xs"].shape[0]
    width = scr["xs"].shape[1]
    half = scr["gate"].shape[1]
    tiles = half // CT
    xs, dys, stage, act, dbr = scr["xs"], scr["dys"], scr["stage"], scr["act"], scr["dbr"]
    vs, gvp, gate, gated, dsp, dgs, dpre = (
        scr["vs"], scr["gvp"], scr["gate"], scr["gated"], scr["dsp"], scr["dgs"], scr["dpre"],
    )
    for m in range(groups):

        @pl.when(me == m)
        def _(m=m):
            for k in range(groups):
                at = (m ^ k) * slot_count
                stage[...] = parcel.at[k, slot][...].astype(F32)
                xs[at : at + slot_count, :] = stage[0:slot_count, :]
                dys[at : at + slot_count, :] = stage[slot_count : 2 * slot_count, :]

    x = xs[0:rows, :]
    mean = jnp.mean(x, axis=-1, keepdims=True)
    cen = x - mean
    inv = lax.rsqrt(jnp.mean(cen * cen, axis=-1, keepdims=True) + EPS)
    xhat = cen * inv
    xs[0:rows, :] = xhat
    scr["inv"][0:rows, :] = jnp.broadcast_to(inv, (rows, 128))
    act[0:rows, :] = (xhat * par["ln_gain"][...] + par["ln_bias"][...]).astype(BF16)
    db = (dys[0:rows, :] * par["live"][kind, :, 0:1]).astype(BF16)
    dbr[0:rows, :] = db
    acc["b_out"][...] += col8(db.astype(F32))

    @pl.loop(0, tiles, unroll=tiles)
    def _(t):
        at = pl.ds(pl.multiple_of(t * CT, CT), CT)
        far = pl.ds(pl.multiple_of(half + t * CT, CT), CT)
        z = dot(act[0:rows, :], par["w_in"][:, far]) + par["b_in"][:, far]
        g, slope = gelu_both(z)
        vs[0:rows, at] = g
        gvp[0:rows, at] = slope.astype(BF16)

    total = fold(vs[0:rows, :])
    vmean = jnp.sum(total, axis=-1, keepdims=True) / half
    cen = vs[0:rows, :] - vmean
    vinv = lax.rsqrt(jnp.sum(fold(cen * cen), axis=-1, keepdims=True) / half + EPS)
    vhat = cen * vinv
    vs[0:rows, :] = vhat
    gate[0:rows, :] = (vhat * par["gate_gain"][...] + par["gate_bias"][...]).astype(BF16)
    last = lax.broadcasted_iota(jnp.int32, (16, 1), 0) == 15
    gate[rows - 16 : rows, :] = jnp.where(last, 1.0, gate[rows - 16 : rows, :].astype(F32)).astype(BF16)
    scr["hs"][0:rows, :] = jnp.zeros((rows, 128), F32)
    scr["hv"][0:rows, :] = jnp.zeros((rows, 128), F32)

    @pl.loop(0, tiles, unroll=tiles)
    def _(t):
        at = pl.ds(pl.multiple_of(t * CT, CT), CT)
        z = dot(act[0:rows, :], par["w_in"][:, at]) + par["b_in"][:, at]
        u, slope = gelu_both(z)
        sp = dot(par["wsp"][kind], gate[0:rows, at]) + par["bsp"][kind, :, 0:1]
        gated[0:rows, at] = (u * sp).astype(BF16)
        dg = dot_nt(dbr[0:rows, :], par["w_out"][at, :])
        pre = (dg * sp * slope).astype(BF16)
        dpre[0:rows, at] = pre
        ds = (dg * u).astype(BF16)
        dsp[0:rows, at] = ds
        dgate = dot(par["wsp_t"][kind], ds)
        vh = vs[0:rows, at]
        acc["gate_bias"][:, at] += col8(dgate)
        acc["gate_gain"][:, at] += col8(dgate * vh)
        h = dgate * par["gate_gain"][:, at]
        dgs[0:rows, at] = h
        scr["hs"][0:rows, :] += fold(h)
        scr["hv"][0:rows, :] += fold(h * vh)

    hmean = jnp.sum(scr["hs"][0:rows, :], axis=-1, keepdims=True) / half
    hvmean = jnp.sum(scr["hv"][0:rows, :], axis=-1, keepdims=True) / half

    @pl.loop(0, tiles, unroll=tiles)
    def _(t):
        at = pl.ds(pl.multiple_of(t * CT, CT), CT)
        far = pl.ds(pl.multiple_of(half + t * CT, CT), CT)
        dv = vinv * (dgs[0:rows, at] - hmean - vs[0:rows, at] * hvmean)
        pre = (dv * gvp[0:rows, at].astype(F32)).astype(BF16)
        dpre[0:rows, far] = pre

    mixed = dot_nt(dsp[0:rows, :], gate[0:rows, :])
    for c in range(acc["w_sp"].shape[0]):
        acc["w_sp"][c, :, 0:rows] += jnp.where(kind == c + 1, mixed, 0.0)
    branch = dot(gated[0:rows, :], par["w_out"][...]) + par["b_out"][...]
    dys[0:rows, :] = branch * KEEP
    dact = dot_nt(dpre[0:rows, :], par["w_in"][...])
    xhat = xs[0:rows, :]
    acc["ln_bias"][...] += col8(dact)
    acc["ln_gain"][...] += col8(dact * xhat)
    h = dact * par["ln_gain"][...]
    back = scr["inv"][0:rows, 0:1] * (
        h - jnp.mean(h, axis=-1, keepdims=True) - xhat * jnp.mean(h * xhat, axis=-1, keepdims=True)
    )
    xs[0:rows, :] = back
    for m in range(groups):

        @pl.when(me == m)
        def _(m=m):
            for k in range(groups):
                at = (m ^ k) * slot_count
                stage[0:slot_count, :] = dys[at : at + slot_count, :]
                stage[slot_count : 2 * slot_count, :] = xs[at : at + slot_count, :]
                parcel[k, slot] = stage[...].astype(BF16)


PAR = ("ln_gain", "ln_bias", "w_in", "b_in", "gate_gain", "gate_bias", "wsp", "wsp_t", "bsp", "live", "pick", "w_out", "b_out")
ACC = ("w_sp", "gate_gain", "gate_bias", "ln_gain", "ln_bias", "b_out", "w_in", "w_out")
SCR = ("stage", "xs", "dys", "inv", "vs", "gvp", "gate", "dsp", "dgs", "hs", "hv")
KEPT = ("act", "dbr", "gated", "dpre")


def reduce_orders(dp):
    bits = [("dp", 1 << b) for b in range(dp.bit_length() - 1)]
    x, z, y = bits[:1], bits[1:], [("patch", 2)]
    return {"a": x + y + z, "b": y + x + z, "c": z + x + y, "d": x + z + y, "e": y + z + x, "f": z + y + x}

def plan_sizes(depth, rows):
    sizes = [rows]
    for _ in range(depth):
        sizes.append(sizes[-1] // 2 if sizes[-1] // 2 >= 16 else sizes[-1])
    return sizes

LINES = ("gate_gain", "gate_bias", "ln_gain", "ln_bias", "b_out")


def gather_gradients(total_ref, par, acc, kept):
    act_t = jnp.concatenate([kept["act"][...].T, jnp.ones((16, kept["act"].shape[0]), BF16)], axis=0)
    for t in range(acc["w_in"].shape[1] // CT):
        at = slice(t * CT, (t + 1) * CT)
        acc["w_in"][:, at] += dot(act_t, kept["dpre"][:, at])
    dbr_t = kept["dbr"][...].T
    for t in range(acc["w_out"].shape[1] // CT):
        at = slice(t * CT, (t + 1) * CT)
        acc["w_out"][:, at] += dot(dbr_t, kept["gated"][:, at])


def lay_out(total_ref, par, acc):
    width, half = acc["w_out"].shape
    wide = acc["w_in"].shape[1]
    base = wide + half
    rows, span = acc["w_sp"].shape[1:]
    total_ref[:, 0:wide] = acc["w_in"][0:width, :].astype(BF16)
    total_ref[:, wide:base] = acc["w_out"][...].astype(BF16)
    mix = acc["w_sp"][2, :, 0:rows]
    for c in range(2):
        pick = par["pick"][c]
        part = dot(acc["w_sp"][c, :, 0:rows].astype(BF16), pick).astype(BF16)
        mix = mix + dot(par["pick"][2 + c], part)
    total_ref[:, base:] = jnp.zeros((width, total_ref.shape[1] - base), BF16)
    total_ref[0:rows, base : base + rows] = mix.astype(BF16)
    lines = []
    for name in LINES:
        v = jnp.sum(acc[name][...], axis=0, keepdims=True)
        lines += [v[:, i * width : (i + 1) * width] for i in range(v.shape[1] // width)]
    lines.append(jnp.zeros((16 - len(lines), width), F32))
    more = [acc["w_in"][width : width + 1, i * width : (i + 1) * width] for i in range(wide // width)]
    more.append(jnp.zeros((16 - len(more), width), F32))
    total_ref[rows : rows + 32, base : base + width] = jnp.concatenate(lines + more, axis=0).astype(BF16)


def layer_kernel(orders, spans, sizes, slot_count, groups, pair, cls_ref, *refs):
    depth = len(orders[0])
    packed, refs = refs[:groups], refs[groups:]
    par, refs = dict(zip(PAR, refs)), refs[len(PAR) :]
    out_ref, back_ref, total_ref, parcel, *refs = refs
    acc, refs = dict(zip(ACC, refs)), refs[len(ACC) :]
    scr, refs = dict(zip(SCR, refs)), refs[len(SCR) :]
    kept, refs = dict(zip(KEPT, refs)), refs[len(KEPT) :]
    first, *refs = refs
    rbufs, refs = refs[:depth], refs[depth:]
    send_sem, recv_sem, in_send, in_recv, back_send, back_recv, own_sem = refs
    dp, patch = lax.axis_index("dp"), lax.axis_index("patch")
    core = patch & 1

    def peer(axis, bit):
        return (dp ^ bit, patch) if axis == "dp" else (dp, patch ^ bit)

    peers = [peer("patch", 1), peer("patch", 3)] + [peer(a, b) for a, b in orders[0]]
    barrier = pltpu.get_barrier_semaphore()
    for other in peers:
        pl.semaphore_signal(barrier, inc=1, device_id=other, device_id_type=MESH)
    pl.semaphore_wait(barrier, len(peers))

    slots = parcel.shape[1]

    def inward(k, j):
        if k == 0:
            return pltpu.make_async_copy(packed[0].at[j], parcel.at[0, j], own_sem.at[0, j])
        return pltpu.make_async_remote_copy(
            src_ref=packed[k].at[j], dst_ref=parcel.at[k, j], send_sem=in_send.at[k, j], recv_sem=in_recv.at[k, j],
            device_id=peer("patch", k), device_id_type=MESH,
        )

    def back(k, j):
        place = j * groups + jnp.where(lax.rem(j, 2) == 0, patch, groups - 1 - patch)
        if k == 0:
            return pltpu.make_async_copy(parcel.at[0, j], back_ref.at[place], own_sem.at[1, j])
        return pltpu.make_async_remote_copy(
            src_ref=parcel.at[k, j], dst_ref=back_ref.at[place], send_sem=back_send.at[k, j], recv_sem=back_recv.at[k, j],
            device_id=peer("patch", k), device_id_type=MESH,
        )

    @pl.loop(0, slots)
    def _(j):
        for k in range(groups - 1, -1, -1):
            inward(k, j).start()

    for ref in acc.values():
        ref[...] = jnp.zeros_like(ref)
    rows = scr["xs"].shape[0]
    for ref in kept.values():
        if ref.shape[0] > pair * rows:
            ref[pair * rows :, :] = jnp.zeros((ref.shape[0] - pair * rows, ref.shape[1]), BF16)
    n = groups * slot_count
    for name in ("xs", "dys"):
        scr[name][rows - 16 : rows, :] = jnp.zeros((16, scr[name].shape[1]), F32)

    @pl.loop(0, slots)
    def _(j):
        for k in range(groups):
            inward(k, j).wait()
        half_at = pl.ds(pl.multiple_of(lax.rem(j, pair) * rows, 16), rows)
        views = {name: ref.at[half_at] for name, ref in kept.items()}
        image_work(cls_ref[j], j, slot_count, patch, parcel, par, acc, scr | views)

        @pl.when(lax.rem(j, pair) == pair - 1)
        def _():
            gather_gradients(total_ref, par, acc, kept)

    lay_out(total_ref, par, acc)
    half = total_ref.shape[1] // 2
    tall = total_ref.shape[0]
    pieces = len(orders)
    mine = pl.multiple_of(core * half, 128)
    theirs = pl.multiple_of((1 - core) * half, 128)
    copies = []

    def send(src, dst, step, i, other):
        copy = pltpu.make_async_remote_copy(
            src_ref=src, dst_ref=dst, send_sem=send_sem.at[step, i], recv_sem=recv_sem.at[step, i], device_id=other,
            device_id_type=MESH,
        )
        copy.start()
        copies.append(copy)
        return copy

    def cols(i):
        return pl.ds(spans[i][0], spans[i][1])

    def shifted(base, i):
        return pl.ds(pl.multiple_of(base + spans[i][0], 128), spans[i][1])

    def high(axis, bit):
        return jnp.where(((dp if axis == "dp" else patch) & bit) != 0, 1, 0)

    def give_back(begin, end):
        @pl.loop(begin, end)
        def _(j):
            for k in range(groups - 1, -1, -1):
                back(k, j).start()

    state = [0] * pieces
    flying = [
        send(total_ref.at[:, shifted(theirs, i)], first.at[:, cols(i)], 0, i, peer("patch", 1)) for i in range(pieces)
    ]
    early = slots * EARLY // 6
    give_back(0, early)
    for s in range(depth + 1):
        for i in range(pieces):
            flying[i].wait_recv()
            lo = state[i]
            if s > 0 and sizes[s - 1] == sizes[s]:
                flying[i].wait_send()
                copies[:] = [copy for copy in copies if copy is not flying[i]]
            got_ref = first if s == 0 else rbufs[s - 1]
            unit = 32 if sizes[s] % 32 == 0 else 16

            @pl.loop(0, sizes[s], step=unit)
            def _(r, i=i, lo=lo, got_ref=got_ref, unit=unit):
                at = pl.ds(pl.multiple_of(lo + r, 16), unit)
                got = pl.ds(pl.multiple_of(r, 16), unit)
                total_ref[at, shifted(mine, i)] = (
                    total_ref[at, shifted(mine, i)].astype(F32) + got_ref[got, cols(i)].astype(F32)
                ).astype(BF16)

            if s < depth:
                axis, bit = orders[i][s]
                keep = sizes[s + 1]
                give = state[i]
                if keep < sizes[s]:
                    give = pl.multiple_of(state[i] + (1 - high(axis, bit)) * keep, 16)
                    state[i] = pl.multiple_of(state[i] + high(axis, bit) * keep, 16)
                flying[i] = send(
                    total_ref.at[pl.ds(give, keep), shifted(mine, i)], rbufs[s].at[pl.ds(0, keep), cols(i)], s + 1, i,
                    peer(axis, bit),
                )
    for i in range(pieces):
        at = pl.ds(pl.multiple_of(state[i], 16), sizes[depth])
        out_ref[at, shifted(mine, i)] = total_ref[at, shifted(mine, i)]
    flying = [None] * pieces
    for s in range(depth, -1, -1):
        if s == depth - 2:
            give_back(early, slots)
        for i in range(pieces):
            if flying[i] is not None:
                flying[i].wait_recv()
                flying[i] = None
            step = 2 * depth + 1 - s
            if s == 0:
                where = out_ref.at[:, shifted(mine, i)]
                flying[i] = send(where, where, step, i, peer("patch", 1))
            elif sizes[s] < sizes[s - 1]:
                axis, bit = orders[i][s - 1]
                where = out_ref.at[pl.ds(pl.multiple_of(state[i], 16), sizes[s]), shifted(mine, i)]
                flying[i] = send(where, where, step, i, peer(axis, bit))
                state[i] = state[i] - high(axis, bit) * sizes[s]
    for i in range(pieces):
        flying[i].wait_recv()

    @pl.loop(0, slots)
    def _(j):
        for k in range(groups):
            back(k, j).wait()

    for copy in copies:
        copy.wait_send()


def call_layer(cls, packed, par, dp, groups, slot_count, pieces):
    slots, stage_rows, width = packed[0].shape
    wide, half, side = par["w_in"].shape[1], par["w_out"].shape[0], par["wsp"].shape[1]
    span = up(side, 128)
    pair = 2 if slots % 2 == 0 else 1
    columns = wide + half + width
    table = reduce_orders(dp)
    orders = [table[name] for name, _ in pieces]
    starts = np.cumsum([0] + [w * 128 for _, w in pieces])
    spans = [(int(starts[i]), w * 128) for i, (_, w) in enumerate(pieces)]
    depth = len(orders[0])
    sizes = plan_sizes(depth, width)
    vmem = pl.BlockSpec(memory_space=pltpu.VMEM)
    far = pl.BlockSpec(memory_space=pl.ANY)
    acc = {
        "w_sp": (3, side, span), "gate_gain": (8, half), "gate_bias": (8, half), "ln_gain": (8, width),
        "ln_bias": (8, width), "b_out": (8, width), "w_in": (width + 16, wide), "w_out": (width, half),
    }
    scr = {
        "stage": ((stage_rows, width), F32), "xs": ((side, width), F32), "dys": ((side, width), F32),
        "inv": ((side, 128), F32), "vs": ((side, half), F32), "gvp": ((side, half), BF16), "gate": ((side, half), BF16),
        "dsp": ((side, half), BF16), "dgs": ((side, half), F32), "hs": ((side, 128), F32), "hv": ((side, 128), F32),
    }
    room = up(pair * side, 256)
    return pl.pallas_call(
        functools.partial(layer_kernel, orders, spans, sizes, slot_count, groups, pair),
        out_shape=[
            jax.ShapeDtypeStruct((width, columns), BF16),
            jax.ShapeDtypeStruct((slots * groups, stage_rows, width), BF16),
        ],
        in_specs=[pl.BlockSpec(memory_space=pltpu.SMEM)] + [far] * groups + [vmem] * len(PAR),
        out_specs=[vmem, far],
        scratch_shapes=[pltpu.VMEM((width, columns), BF16), pltpu.VMEM((groups, slots, stage_rows, width), BF16)]
        + [pltpu.VMEM(acc[name], F32) for name in ACC]
        + [pltpu.VMEM(*scr[name]) for name in SCR]
        + [pltpu.VMEM((room, n), BF16) for n in (width, width, half, wide)]
        + [pltpu.VMEM((width, columns // 2), BF16)]
        + [pltpu.VMEM((size, columns // 2), BF16) for size in sizes[1:]]
        + [pltpu.SemaphoreType.DMA((2 * depth + 2, len(pieces)))] * 2
        + [pltpu.SemaphoreType.DMA((groups, slots))] * 4
        + [pltpu.SemaphoreType.DMA((2, slots))],
        compiler_params=pltpu.CompilerParams(
            collective_id=1, has_side_effects=True, vmem_limit_bytes=64 * 1024 * 1024 - 65536
        ),
        name="layer",
    )(cls, *packed, *[par[name] for name in PAR])


def local(images, cotangent, res_class, skip, ln_gain, ln_bias, w_in, b_in, gate_gain, gate_bias, w_spatial, b_spatial, w_out, b_out):
    groups = lax.axis_size("patch")
    dp = lax.axis_size("dp")
    count, slot_count, width = images.shape
    half = w_out.shape[0]
    wide = w_in.shape[1]
    slots = count // groups
    quarter = tuple(side * side // groups for side in SIDES)
    patches = groups * slot_count
    side = up(patches, 16)
    span = up(patches, 128)
    stage_rows = up(2 * slot_count, 16)
    me = lax.axis_index("patch").astype(jnp.int32)

    key = jnp.where(skip != 0, res_class + 1, 0).astype(jnp.int32)
    index = jnp.arange(count, dtype=jnp.int32)
    before = (key[None, :] > key[:, None]) | ((key[None, :] == key[:, None]) & (index[None, :] < index[:, None]))
    rank = jnp.sum(before.astype(jnp.int32), axis=1)
    hit = rank[None, :] == index[:, None]
    order = jnp.sum(jnp.where(hit, index[None, :], 0), axis=1)
    slot_index = jnp.arange(slots, dtype=jnp.int32)
    spot = slot_index * groups + jnp.where(slot_index % 2 == 0, me, groups - 1 - me)
    cls = jnp.sum(jnp.where(spot[:, None] == rank[None, :], key[None, :], 0), axis=1)
    me1 = me.reshape(1)

    whole = pl.BlockSpec(memory_space=pltpu.VMEM)
    smem = pl.BlockSpec(memory_space=pltpu.SMEM)
    img_t = jnp.swapaxes(images, 0, 1)
    cot_t = jnp.swapaxes(cotangent, 0, 1)
    planes = (width // 128, slot_count * count, 128)
    packed = pl.pallas_call(
        functools.partial(pack_kernel, slot_count, groups),
        out_shape=[jax.ShapeDtypeStruct((slots, stage_rows, width), BF16)] * groups,
        in_specs=[smem, smem, whole, whole],
        out_specs=[whole] * groups,
        scratch_shapes=[pltpu.VMEM(planes, F32), pltpu.VMEM(planes, F32), pltpu.VMEM((stage_rows, width), F32)],
        compiler_params=pltpu.CompilerParams(vmem_limit_bytes=40 * 1024 * 1024),
        name="pack",
    )(me1, order, img_t, cot_t)

    live, where = [], []
    at = jnp.arange(side, dtype=jnp.int32)
    place, within = at // slot_count, at % slot_count
    for q in quarter:
        live.append((within < q) & (at < patches))
        where.append(jnp.where(live[-1], place * q + within, -1))
    picks = [(w[:, None] == at[None, :]).astype(BF16) for w in where]
    w_pad = jnp.pad(w_spatial, ((0, side - patches),) * 2)
    b_pad = jnp.pad(b_spatial, (0, side - patches))
    spread = [jnp.zeros((side, side), BF16)]
    bias = [jnp.zeros((side,), F32)]
    for c, pick in enumerate(picks):
        if c < 2:
            moved = jnp.einsum("ta,ab->tb", pick, w_pad, preferred_element_type=F32).astype(BF16)
            spread.append(jnp.einsum("tb,sb->ts", moved, pick, preferred_element_type=F32).astype(BF16))
            bias.append(jnp.sum(jnp.where(where[c][:, None] == at[None, :], b_pad[None, :], 0.0), axis=1))
        else:
            spread.append(w_pad)
            bias.append(b_pad)
    wsp = jnp.stack(spread)
    wsp_t = jnp.swapaxes(wsp, 1, 2)
    bsp = jnp.stack([jnp.broadcast_to(v[:, None], (side, 128)) for v in bias])
    keep = jnp.stack([jnp.zeros((side, 128), F32)] + [jnp.broadcast_to(jnp.where(v, KEEP, 0.0)[:, None], (side, 128)) for v in live])
    corner = ((at[:, None] == side - 1) & (at[None, :] == side - 1)).astype(BF16)
    lift = [pick + corner for pick in picks[:2]]
    pick = jnp.stack(lift + [v.T for v in lift])
    par = {
        "ln_gain": ln_gain[None, :], "ln_bias": ln_bias[None, :], "w_in": w_in, "b_in": b_in[None, :],
        "gate_gain": gate_gain[None, :], "gate_bias": gate_bias[None, :], "wsp": wsp, "wsp_t": wsp_t, "bsp": bsp, "live": keep, "pick": pick,
        "w_out": w_out, "b_out": b_out[None, :],
    }
    summed, backs = call_layer(cls, packed, par, dp, groups, slot_count, PIECES)
    out_t, grad_t = pl.pallas_call(
        functools.partial(unpack_kernel, slot_count, quarter),
        out_shape=[jax.ShapeDtypeStruct((slot_count, count, width), BF16), jax.ShapeDtypeStruct((slot_count, count, width), F32)],
        in_specs=[smem, smem] + [whole] * 3,
        out_specs=[whole, whole],
        scratch_shapes=[pltpu.VMEM(planes, F32), pltpu.VMEM(planes, F32), pltpu.VMEM((stage_rows, width), F32)],
        compiler_params=pltpu.CompilerParams(vmem_limit_bytes=40 * 1024 * 1024),
        name="unpack",
    )(rank, key, img_t, cot_t, backs)
    output = jnp.swapaxes(out_t, 0, 1)
    grad_images = jnp.swapaxes(grad_t, 0, 1)

    cut = 2 * CT
    first, last = wide // cut, (wide + half) // cut
    g_w_in, g_w_out = pl.pallas_call(
        functools.partial(widen_kernel, first),
        out_shape=[jax.ShapeDtypeStruct((width, wide), F32), jax.ShapeDtypeStruct((half, width), F32)],
        grid=(last,),
        in_specs=[pl.BlockSpec((width, cut), lambda t: (0, t))],
        out_specs=[
            pl.BlockSpec((width, cut), lambda t: (0, jnp.minimum(t, first - 1))),
            pl.BlockSpec((cut, width), lambda t: (jnp.maximum(t - first, 0), 0)),
        ],
        name="widen",
    )(summed)
    base = wide + half
    small = summed[0 : side + 32, base:].astype(F32)
    lines = small[side : side + 16].reshape(-1)
    ends = np.cumsum([0, half, half, width, width, width])
    g_gate_gain, g_gate_bias, g_ln_gain, g_ln_bias, g_b_out = [lines[ends[i] : ends[i + 1]] for i in range(5)]
    g_b_in = small[side + 16 : side + 32].reshape(-1)[:wide]
    return (
        output, grad_images, g_ln_gain, g_ln_bias, g_w_in, g_b_in, g_gate_gain, g_gate_bias,
        small[:patches, :patches], small[:patches, side - 1], g_w_out, g_b_out,
    )


def solution(mesh):
    placed = (P("dp", "patch", None),) * 2 + (P("dp"),) * 2 + (P(),) * 10
    return jax.shard_map(
        local, mesh=mesh, in_specs=placed, out_specs=(P("dp", "patch", None),) * 2 + (P(),) * 10, check_vma=False,
    )
```

```python
import functools

import jax
import jax.numpy as jnp
import numpy as np
from jax import lax
from jax.experimental import pallas as pl
from jax.experimental.pallas import tpu as pltpu
from jax.sharding import PartitionSpec as P

MESH = pl.DeviceIdType.MESH
SIDES = (10, 14, 18)
EPS = 1e-05
F32 = jnp.float32
BF16 = jnp.bfloat16
CT = 256
BACKS = (4, 4, 4, 5)
PIECES = (("c", 1), ("d", 2), ("b", 2)) * 4
KEEP = np.float32(1.0) / np.float32(0.9)
GELU_C = np.float32(np.sqrt(2.0 / np.pi))
GELU_K = np.float32(0.044715)


def up(value, unit):
    return -(-value // unit) * unit


def dot(a, b):
    return lax.dot_general(a, b, (((1,), (0,)), ((), ())), preferred_element_type=F32)


def dot_nt(a, b):
    return lax.dot_general(a, b, (((1,), (1,)), ((), ())), preferred_element_type=F32)


def dot_tn(a, b):
    return lax.dot_general(a, b, (((0,), (0,)), ((), ())), preferred_element_type=F32)


def gelu_both(z):
    z2 = z * z
    t = jnp.tanh(z * (GELU_C + (GELU_C * GELU_K) * z2))
    a = 0.5 + 0.5 * t
    g = z * a
    slope = a + (g * (1.0 - t)) * (GELU_C + (3.0 * GELU_C * GELU_K) * z2)
    return g, slope


def fold(v):
    total = v[:, :128]
    for i in range(1, v.shape[1] // 128):
        total = total + v[:, i * 128 : (i + 1) * 128]
    return total


def col8(v):
    return jnp.sum(v.reshape(v.shape[0] // 8, 8, v.shape[1]), axis=0)


def pack_kernel(slot_count, groups, me_ref, order_ref, img_ref, cot_ref, *refs):
    outs, (hold, xf, yf, stage, sem) = refs[:-5], refs[-5:]
    me = me_ref[0]
    count = img_ref.shape[1]
    lanes = xf.shape[0]

    @pl.loop(0, slot_count, unroll=9)
    def _(r):
        at = pl.ds(pl.multiple_of(r * count, 8), count)
        for c in range(lanes):
            xf[c, at, :] = img_ref[r, :, c * 128 : (c + 1) * 128].astype(F32)
            yf[c, at, :] = cot_ref[r, :, c * 128 : (c + 1) * 128].astype(F32)

    @pl.loop(0, outs[0].shape[0])
    def _(j):
        for k in range(groups):
            dest = me ^ k
            which = order_ref[j * groups + jnp.where(lax.rem(j, 2) == 0, dest, groups - 1 - dest)]
            for c in range(lanes):
                cols = slice(c * 128, (c + 1) * 128)
                stage[0:slot_count, cols] = xf[c, pl.ds(which, slot_count, stride=count), :]
                stage[slot_count : 2 * slot_count, cols] = yf[c, pl.ds(which, slot_count, stride=count), :]
            hold[k, j] = stage[...].astype(BF16)
            pltpu.make_async_copy(hold.at[k, j], outs[k].at[j], sem.at[k, j]).start()

    @pl.loop(0, outs[0].shape[0])
    def _(j):
        for k in range(groups):
            pltpu.make_async_copy(hold.at[k, j], outs[k].at[j], sem.at[k, j]).wait()


def finish_kernel(slot_count, quarter, wide, half, rank_ref, key_ref, img_far, cot_far, back_far, src_ref, *refs):
    in_ref, out_w_ref, w_sp_ref, b_sp_ref, *refs = refs
    lines, (out_ref, grad_ref, xf, yf, stage, out, grad, img_ref, cot_ref, back_ref, sem) = refs[:-11], refs[-11:]
    lanes = xf.shape[0]
    count = img_ref.shape[1]
    width, cut = src_ref.shape
    t = pl.program_id(0)
    small, first = 0, 1
    last = first + (wide + half) // cut
    part = -(-count // (last - 4))
    copies = [pltpu.make_async_copy(out, out_ref, sem.at[0]), pltpu.make_async_copy(grad, grad_ref, sem.at[1])]
    loads = [
        pltpu.make_async_copy(a, b, sem.at[2 + i])
        for i, (a, b) in enumerate(((img_far, img_ref), (cot_far, cot_ref), (back_far, back_ref)))
    ]

    @pl.when(t == small)
    def _():
        for load in loads:
            load.start()
        block = src_ref[...].astype(F32)
        patches = w_sp_ref.shape[0]
        side = up(patches, 16)
        w_sp_ref[...] = block[:patches, :patches]
        low = (side - 1) // 128 * 128
        b_sp_ref[...] = block[:side, low : low + 128].T[side - 1 - low, :patches]
        at = side
        for ref in lines:
            for n in range(ref.shape[0] // width):
                ref[n * width : (n + 1) * width] = block[at, :]
                at += 1

    @pl.when(t == first)
    def _():
        for load in loads:
            load.wait()

        @pl.loop(0, slot_count, unroll=9)
        def _(r):
            at = pl.ds(pl.multiple_of(r * count, 8), count)
            for c in range(lanes):
                xf[c, at, :] = img_ref[r, :, c * 128 : (c + 1) * 128].astype(F32)
                yf[c, at, :] = cot_ref[r, :, c * 128 : (c + 1) * 128].astype(F32)

    @pl.when((t >= first) & (t < first + wide // cut))
    def _():
        in_ref[...] = src_ref[...].astype(F32)

    @pl.when(t >= first + wide // cut)
    def _():
        out_w_ref[...] = src_ref[...].astype(F32).T

    @pl.loop(jnp.clip((t - 2) * part, 0, count), jnp.clip((t - 1) * part, 0, count))
    def _(i):
        key = key_ref[i]
        for c, q in enumerate(quarter):

            @pl.when(key == c + 1)
            def _(q=q):
                stage[...] = back_ref[rank_ref[i]].astype(F32)
                at = pl.ds(i, q, stride=count)
                for b in range(lanes):
                    cols = slice(b * 128, (b + 1) * 128)
                    xf[b, at, :] = xf[b, at, :] + stage[0:q, cols]
                    yf[b, at, :] = yf[b, at, :] + stage[slot_count : slot_count + q, cols]

    @pl.when(t == last - 2)
    def _():
        @pl.loop(0, slot_count, unroll=9)
        def _(r):
            at = pl.ds(pl.multiple_of(r * count, 8), count)
            for c in range(lanes):
                out[r, :, c * 128 : (c + 1) * 128] = xf[c, at, :].astype(BF16)
                grad[r, :, c * 128 : (c + 1) * 128] = yf[c, at, :]

        for copy in copies:
            copy.start()

    @pl.when(t == last - 1)
    def _():
        for copy in copies:
            copy.wait()


def image_work(kind, slot, slot_count, me, parcel, par, acc, scr):
    groups = parcel.shape[0]
    rows = scr["xs"].shape[0]
    width = scr["xs"].shape[1]
    half = scr["gate"].shape[1]
    tiles = half // CT
    xs, dys, stage, act, dbr = scr["xs"], scr["dys"], scr["stage"], scr["act"], scr["dbr"]
    vs, gvp, gate, gated, dsp, dgs, dpre = (
        scr["vs"], scr["gvp"], scr["gate"], scr["gated"], scr["dsp"], scr["dgs"], scr["dpre"],
    )
    for m in range(groups):

        @pl.when(me == m)
        def _(m=m):
            for k in range(groups):
                at = (m ^ k) * slot_count
                stage[...] = parcel.at[k, slot][...].astype(F32)
                xs[at : at + slot_count, :] = stage[0:slot_count, :]
                dys[at : at + slot_count, :] = stage[slot_count : 2 * slot_count, :]

    x = xs[0:rows, :]
    mean = jnp.mean(x, axis=-1, keepdims=True)
    cen = x - mean
    inv = lax.rsqrt(jnp.mean(cen * cen, axis=-1, keepdims=True) + EPS)
    xhat = cen * inv
    xs[0:rows, :] = xhat
    scr["inv"][0:rows, :] = jnp.broadcast_to(inv, (rows, 128))
    act[0:rows, :] = (xhat * par["ln_gain"][...] + par["ln_bias"][...]).astype(BF16)
    db = (dys[0:rows, :] * par["live"][kind, :, 0:1]).astype(BF16)
    dbr[0:rows, :] = db
    acc["b_out"][...] += col8(db.astype(F32))

    @pl.loop(0, tiles, unroll=tiles)
    def _(t):
        at = pl.ds(pl.multiple_of(t * CT, CT), CT)
        far = pl.ds(pl.multiple_of(half + t * CT, CT), CT)
        z = dot(act[0:rows, :], par["w_in"][:, far]) + par["b_in"][:, far]
        g, slope = gelu_both(z)
        vs[0:rows, at] = g
        gvp[0:rows, at] = slope.astype(BF16)

    total = fold(vs[0:rows, :])
    vmean = jnp.sum(total, axis=-1, keepdims=True) / half
    cen = vs[0:rows, :] - vmean
    vinv = lax.rsqrt(jnp.sum(fold(cen * cen), axis=-1, keepdims=True) / half + EPS)
    vhat = cen * vinv
    vs[0:rows, :] = vhat
    gate[0:rows, :] = (vhat * par["gate_gain"][...] + par["gate_bias"][...]).astype(BF16)
    last = lax.broadcasted_iota(jnp.int32, (16, 1), 0) == 15
    gate[rows - 16 : rows, :] = jnp.where(last, 1.0, gate[rows - 16 : rows, :].astype(F32)).astype(BF16)
    scr["hs"][0:rows, :] = jnp.zeros((rows, 128), F32)
    scr["hv"][0:rows, :] = jnp.zeros((rows, 128), F32)

    @pl.loop(0, tiles, unroll=tiles)
    def _(t):
        at = pl.ds(pl.multiple_of(t * CT, CT), CT)
        z = dot(act[0:rows, :], par["w_in"][:, at]) + par["b_in"][:, at]
        u, slope = gelu_both(z)
        sp = dot(par["wsp"][kind], gate[0:rows, at]) + par["bsp"][kind, :, 0:1]
        gated[0:rows, at] = (u * sp).astype(BF16)
        dg = dot_nt(dbr[0:rows, :], par["w_out"][at, :])
        pre = (dg * sp * slope).astype(BF16)
        dpre[0:rows, at] = pre
        ds = (dg * u).astype(BF16)
        dsp[0:rows, at] = ds
        dgate = dot(par["wsp_t"][kind], ds)
        vh = vs[0:rows, at]
        acc["gate_bias"][:, at] += col8(dgate)
        acc["gate_gain"][:, at] += col8(dgate * vh)
        h = dgate * par["gate_gain"][:, at]
        dgs[0:rows, at] = h
        scr["hs"][0:rows, :] += fold(h)
        scr["hv"][0:rows, :] += fold(h * vh)

    hmean = jnp.sum(scr["hs"][0:rows, :], axis=-1, keepdims=True) / half
    hvmean = jnp.sum(scr["hv"][0:rows, :], axis=-1, keepdims=True) / half

    @pl.loop(0, tiles, unroll=tiles)
    def _(t):
        at = pl.ds(pl.multiple_of(t * CT, CT), CT)
        far = pl.ds(pl.multiple_of(half + t * CT, CT), CT)
        dv = vinv * (dgs[0:rows, at] - hmean - vs[0:rows, at] * hvmean)
        pre = (dv * gvp[0:rows, at].astype(F32)).astype(BF16)
        dpre[0:rows, far] = pre

    mixed = dot_nt(dsp[0:rows, :], gate[0:rows, :])
    for c in range(acc["w_sp"].shape[0]):
        acc["w_sp"][c, :, 0:rows] += jnp.where(kind == c + 1, mixed, 0.0)
    branch = dot(gated[0:rows, :], par["w_out"][...]) + par["b_out"][...]
    dys[0:rows, :] = branch * KEEP
    dact = dot_nt(dpre[0:rows, :], par["w_in"][...])
    xhat = xs[0:rows, :]
    acc["ln_bias"][...] += col8(dact)
    acc["ln_gain"][...] += col8(dact * xhat)
    h = dact * par["ln_gain"][...]
    back = scr["inv"][0:rows, 0:1] * (
        h - jnp.mean(h, axis=-1, keepdims=True) - xhat * jnp.mean(h * xhat, axis=-1, keepdims=True)
    )
    xs[0:rows, :] = back
    for m in range(groups):

        @pl.when(me == m)
        def _(m=m):
            for k in range(groups):
                at = (m ^ k) * slot_count
                stage[0:slot_count, :] = dys[at : at + slot_count, :]
                stage[slot_count : 2 * slot_count, :] = xs[at : at + slot_count, :]
                parcel[k, slot] = stage[...].astype(BF16)


VECTORS = ("b_in", "gate_gain", "gate_bias", "ln_gain", "ln_bias", "b_out", "b_sp")
LARGE = ("w_in", "w_out")
TABLES = ("wsp", "wsp_t", "bsp", "live", "pick")
ACC = ("w_sp", "gate_gain", "gate_bias", "ln_gain", "ln_bias", "b_out", "w_in", "w_out")
SCR = ("stage", "xs", "dys", "inv", "vs", "gvp", "gate", "dsp", "dgs", "hs", "hv")
KEPT = ("act", "dbr", "gated", "dpre")


def reduce_orders(dp):
    bits = [1 << b for b in range(dp.bit_length() - 1)]
    x, z, y = [("dp", bits[:1])], [("dp", [bit]) for bit in bits[1:3]], [("patch", [2])]
    rest = [("dp", [bit]) for bit in bits[3:]]
    return {
        "a": x + y + z + rest, "b": y + x + z + rest, "c": z + x + y + rest, "d": x + z + y + rest, "e": y + z + x + rest,
    }


def combos(bits):
    masks = [0]
    for bit in bits:
        masks += [mask | bit for mask in masks]
    return masks[1:]


def plan_sizes(order, rows):
    sizes = [rows]
    for _, bits in order:
        keep = sizes[-1] >> len(bits)
        sizes.append(keep if keep >= 16 else sizes[-1])
    return sizes


LINES = ("gate_gain", "gate_bias", "ln_gain", "ln_bias", "b_out")


def fill_tables(par, quarter, slot_count, groups):
    side = par["w_sp"].shape[0]
    t = lax.broadcasted_iota(jnp.int32, (side, 1), 0)
    lane = lax.broadcasted_iota(jnp.int32, (1, side), 1)
    place = sum(jnp.where(t >= slot_count * g, 1, 0) for g in range(1, groups))
    within = t - slot_count * place
    w = par["w_sp"][...]
    for name in ("wsp", "wsp_t", "bsp", "live"):
        par[name][0] = jnp.zeros(par[name].shape[1:], par[name].dtype)
    for c, q in enumerate(quarter):
        live = (within < q) & (t < slot_count * groups)
        hit = live & (place * q + within == lane)
        pick = jnp.where(hit, 1.0, 0.0)
        low = pick.astype(BF16)
        par["wsp"][c + 1] = dot_nt(dot(low, w).astype(BF16), low).astype(BF16)
        par["wsp_t"][c + 1] = dot_nt(dot_nt(low, w).astype(BF16), low).astype(BF16)
        bias = jnp.sum(jnp.where(hit, par["b_sp"][...], 0.0), axis=-1, keepdims=True)
        par["bsp"][c + 1] = jnp.broadcast_to(bias, (side, 128))
        par["live"][c + 1] = jnp.broadcast_to(jnp.where(live, KEEP, 0.0), (side, 128))
        if c < 2:
            corner = (t == side - 1) & (lane == side - 1)
            par["pick"][c] = (pick + jnp.where(corner, 1.0, 0.0)).astype(BF16)


def gather_gradients(total_ref, par, acc, kept):
    act_t = jnp.concatenate([kept["act"][...].T, jnp.ones((16, kept["act"].shape[0]), BF16)], axis=0)
    for t in range(acc["w_in"].shape[1] // CT):
        at = slice(t * CT, (t + 1) * CT)
        acc["w_in"][:, at] += dot(act_t, kept["dpre"][:, at])
    dbr_t = kept["dbr"][...].T
    for t in range(acc["w_out"].shape[1] // CT):
        at = slice(t * CT, (t + 1) * CT)
        acc["w_out"][:, at] += dot(dbr_t, kept["gated"][:, at])


def lay_out(total_ref, par, acc):
    width, half = acc["w_out"].shape
    wide = acc["w_in"].shape[1]
    base = wide + half
    rows, span = acc["w_sp"].shape[1:]
    total_ref[:, 0:wide] = acc["w_in"][0:width, :].astype(BF16)
    total_ref[:, wide:base] = acc["w_out"][...].astype(BF16)
    mix = acc["w_sp"][2, :, 0:rows]
    for c in range(2):
        pick = par["pick"][c]
        part = dot(acc["w_sp"][c, :, 0:rows].astype(BF16), pick).astype(BF16)
        mix = mix + dot_tn(pick, part)
    total_ref[:, base:] = jnp.zeros((width, total_ref.shape[1] - base), BF16)
    total_ref[0:rows, base : base + rows] = mix.astype(BF16)
    lines = []
    for name in LINES:
        v = jnp.sum(acc[name][...], axis=0, keepdims=True)
        lines += [v[:, i * width : (i + 1) * width] for i in range(v.shape[1] // width)]
    more = [acc["w_in"][width : width + 1, i * width : (i + 1) * width] for i in range(wide // width)]
    more.append(jnp.zeros((32 - len(lines) - len(more), width), F32))
    total_ref[rows : rows + 32, base : base + width] = jnp.concatenate(lines + more, axis=0).astype(BF16)


def layer_kernel(orders, spans, sizes, slot_count, groups, quarter, lengths, pair, cls_ref, *refs):
    depth = len(orders[0])
    packed, refs = refs[:groups], refs[groups:]
    weights, w_sp_ref, vector_ref, *refs = refs[:2], *refs[2:]
    out_ref, back_ref, total_ref, parcel, *refs = refs
    names = TABLES + LARGE + VECTORS
    par, refs = {"w_sp": w_sp_ref} | dict(zip(names, refs)), refs[len(names) :]
    acc, refs = dict(zip(ACC, refs)), refs[len(ACC) :]
    scr, refs = dict(zip(SCR, refs)), refs[len(SCR) :]
    kept, refs = dict(zip(KEPT, refs)), refs[len(KEPT) :]
    first, *refs = refs
    rbufs, refs = refs[:depth], refs[depth:]
    send_sem, recv_sem, in_send, in_recv, back_send, back_recv, own_sem, load_sem = refs
    dp, patch = lax.axis_index("dp"), lax.axis_index("patch")
    core = patch & 1

    def peer(axis, bit):
        return (dp ^ bit, patch) if axis == "dp" else (dp, patch ^ bit)

    peers = [peer("patch", 1), peer("patch", 3)] + [peer(a, mask) for a, bits in orders[0] for mask in combos(bits)]
    barrier = pltpu.get_barrier_semaphore()
    for other in peers:
        pl.semaphore_signal(barrier, inc=1, device_id=other, device_id_type=MESH)
    pl.semaphore_wait(barrier, len(peers))

    slots = parcel.shape[1]

    def inward(k, j):
        if k == 0:
            return pltpu.make_async_copy(packed[0].at[j], parcel.at[0, j], own_sem.at[0, j])
        return pltpu.make_async_remote_copy(
            src_ref=packed[k].at[j], dst_ref=parcel.at[k, j], send_sem=in_send.at[k, j], recv_sem=in_recv.at[k, j],
            device_id=peer("patch", k), device_id_type=MESH,
        )

    def back(k, j):
        place = j * groups + jnp.where(lax.rem(j, 2) == 0, patch, groups - 1 - patch)
        if k == 0:
            return pltpu.make_async_copy(parcel.at[0, j], back_ref.at[place], own_sem.at[1, j])
        return pltpu.make_async_remote_copy(
            src_ref=parcel.at[k, j], dst_ref=back_ref.at[place], send_sem=back_send.at[k, j], recv_sem=back_recv.at[k, j],
            device_id=peer("patch", k), device_id_type=MESH,
        )

    def give_back(begin, end):
        @pl.loop(begin, end)
        def _(j):
            for k in range(groups - 1, -1, -1):
                back(k, j).start()

    stops = [slots * n // 6 for n in (0, *BACKS, 6)]

    @pl.loop(0, slots)
    def _(j):
        for k in range(groups - 1, -1, -1):
            inward(k, j).start()

    loads = [pltpu.make_async_copy(weights[i], par[name], load_sem.at[i]) for i, name in enumerate(LARGE)]
    for load in loads:
        load.start()
    line = 0
    for name in VECTORS:
        length = par[name].shape[1]
        for begin in range(0, length, vector_ref.shape[1]):
            stop = min(length, begin + vector_ref.shape[1])
            par[name][:, begin:stop] = vector_ref[line : line + 1, 0 : stop - begin]
            line += 1
    fill_tables(par, quarter, slot_count, groups)
    for ref in acc.values():
        ref[...] = jnp.zeros_like(ref)
    rows = scr["xs"].shape[0]
    for ref in kept.values():
        if ref.shape[0] > pair * rows:
            ref[pair * rows :, :] = jnp.zeros((ref.shape[0] - pair * rows, ref.shape[1]), BF16)
    n = groups * slot_count
    for name in ("xs", "dys"):
        scr[name][rows - 16 : rows, :] = jnp.zeros((16, scr[name].shape[1]), F32)
    for load in loads:
        load.wait()

    @pl.loop(0, slots)
    def _(j):
        for k in range(groups):
            inward(k, j).wait()

        @pl.when(j == slots - 2)
        def _():
            give_back(stops[0], stops[1])

        @pl.when(j == slots - 1)
        def _():
            give_back(stops[1], stops[2])

        half_at = pl.ds(pl.multiple_of(lax.rem(j, pair) * rows, 16), rows)
        views = {name: ref.at[half_at] for name, ref in kept.items()}
        image_work(cls_ref[j], j, slot_count, patch, parcel, par, acc, scr | views)

        @pl.when(lax.rem(j, pair) == pair - 1)
        def _():
            gather_gradients(total_ref, par, acc, kept)

    lay_out(total_ref, par, acc)
    half = total_ref.shape[1] // 2
    tall = total_ref.shape[0]
    pieces = len(orders)
    mine = pl.multiple_of(core * half, 128)
    theirs = pl.multiple_of((1 - core) * half, 128)
    copies = []

    def send(src, dst, step, i, part, other):
        copy = pltpu.make_async_remote_copy(
            src_ref=src, dst_ref=dst, send_sem=send_sem.at[part, step, i], recv_sem=recv_sem.at[part, step, i], device_id=other,
            device_id_type=MESH,
        )
        copy.start()
        copies.append(copy)
        return copy

    def cols(i):
        return pl.ds(spans[i][0], spans[i][1])

    def shifted(base, i):
        return pl.ds(pl.multiple_of(base + spans[i][0], 128), spans[i][1])

    def rank_in(axis, bits):
        index = dp if axis == "dp" else patch
        return sum(jnp.where((index & bit) != 0, 1 << n, 0) for n, bit in enumerate(bits))

    def other_rank(axis, bits, mask):
        index = (dp if axis == "dp" else patch) ^ mask
        return sum(jnp.where((index & bit) != 0, 1 << n, 0) for n, bit in enumerate(bits))

    def rows_at(begin, size):
        return pl.ds(pl.multiple_of(begin, 16), size)

    state = [0] * pieces
    flying = [
        [send(total_ref.at[:, shifted(theirs, i)], first.at[:, cols(i)], 0, i, 0, peer("patch", 1))] for i in range(pieces)
    ]
    give_back(stops[2], stops[3])
    for s in range(depth + 1):
        if s == 2:
            give_back(stops[3], stops[4])
        for i in range(pieces):
            size = sizes[i][s]
            for copy in flying[i]:
                copy.wait_recv()
            lo = state[i]
            if s > 0 and sizes[i][s - 1] == size:
                for copy in flying[i]:
                    copy.wait_send()
                copies[:] = [copy for copy in copies if all(copy is not old for old in flying[i])]
            got_ref = first if s == 0 else rbufs[s - 1]
            unit = 32 if size % 32 == 0 else 16

            @pl.loop(0, size, step=unit)
            def _(r, i=i, lo=lo, got_ref=got_ref, unit=unit, size=size, parts=len(flying[i])):
                at = rows_at(lo + r, unit)
                value = total_ref[at, shifted(mine, i)].astype(F32)
                for part in range(parts):
                    value = value + got_ref[rows_at(part * size + r, unit), cols(i)].astype(F32)
                total_ref[at, shifted(mine, i)] = value.astype(BF16)

            if s < depth:
                axis, bits = orders[i][s]
                keep = sizes[i][s + 1]
                base = state[i]
                split = keep < size
                if split:
                    state[i] = base + rank_in(axis, bits) * keep
                flying[i] = []
                for part, mask in enumerate(combos(bits)):
                    give = base + other_rank(axis, bits, mask) * keep if split else base
                    flying[i].append(
                        send(
                            total_ref.at[rows_at(give, keep), shifted(mine, i)],
                            rbufs[s].at[pl.ds(part * keep, keep), cols(i)], s + 1, i, part, peer(axis, mask),
                        )
                    )
    for i in range(pieces):
        at = rows_at(state[i], sizes[i][depth])
        out_ref[at, shifted(mine, i)] = total_ref[at, shifted(mine, i)]
    flying = [[] for _ in range(pieces)]
    for s in range(depth, -1, -1):
        if s == depth - 1:
            give_back(stops[4], stops[5])
        for i in range(pieces):
            for copy in flying[i]:
                copy.wait_recv()
            flying[i] = []
            step = 2 * depth + 1 - s
            if s == 0:
                where = out_ref.at[:, shifted(mine, i)]
                flying[i] = [send(where, where, step, i, 0, peer("patch", 1))]
            elif sizes[i][s] < sizes[i][s - 1]:
                axis, bits = orders[i][s - 1]
                where = out_ref.at[rows_at(state[i], sizes[i][s]), shifted(mine, i)]
                for part, mask in enumerate(combos(bits)):
                    flying[i].append(send(where, where, step, i, part, peer(axis, mask)))
                state[i] = state[i] - rank_in(axis, bits) * sizes[i][s]
    for i in range(pieces):
        for copy in flying[i]:
            copy.wait_recv()

    @pl.loop(0, slots)
    def _(j):
        for k in range(groups):
            back(k, j).wait()

    for copy in copies:
        copy.wait_send()


def call_layer(cls, packed, w_in, w_out, w_pad, vectors, lengths, dp, groups, slot_count, quarter, pieces):
    slots, stage_rows, width = packed[0].shape
    wide, half, side = w_in.shape[1], w_out.shape[0], w_pad.shape[0]
    span = up(side, 128)
    pair = 2 if slots % 2 == 0 else 1
    columns = wide + half + width
    table = reduce_orders(dp)
    orders = [table[name] for name, _ in pieces]
    starts = np.cumsum([0] + [w * 128 for _, w in pieces])
    spans = [(int(starts[i]), w * 128) for i, (_, w) in enumerate(pieces)]
    depth = len(orders[0])
    sizes = [plan_sizes(order, width) for order in orders]
    room_for = [
        max(len(combos(order[s][1])) * size[s + 1] for order, size in zip(orders, sizes)) for s in range(depth)
    ]
    fan = max(len(combos(bits)) for _, bits in orders[0])
    vmem = pl.BlockSpec(memory_space=pltpu.VMEM)
    far = pl.BlockSpec(memory_space=pl.ANY)
    acc = {
        "w_sp": (3, side, span), "gate_gain": (8, half), "gate_bias": (8, half), "ln_gain": (8, width),
        "ln_bias": (8, width), "b_out": (8, width), "w_in": (width + 16, wide), "w_out": (width, half),
    }
    scr = {
        "stage": ((stage_rows, width), F32), "xs": ((side, width), F32), "dys": ((side, width), F32),
        "inv": ((side, 128), F32), "vs": ((side, half), F32), "gvp": ((side, half), BF16), "gate": ((side, half), BF16),
        "dsp": ((side, half), BF16), "dgs": ((side, half), F32), "hs": ((side, 128), F32), "hv": ((side, 128), F32),
    }
    room = up(pair * side, 256)
    return pl.pallas_call(
        functools.partial(layer_kernel, orders, spans, sizes, slot_count, groups, quarter, lengths, pair),
        out_shape=[
            jax.ShapeDtypeStruct((width, columns), BF16),
            jax.ShapeDtypeStruct((slots * groups, stage_rows, width), BF16),
        ],
        in_specs=[pl.BlockSpec(memory_space=pltpu.SMEM)] + [far] * groups + [far, far, vmem, vmem],
        out_specs=[vmem, far],
        scratch_shapes=[pltpu.VMEM((width, columns), BF16), pltpu.VMEM((groups, slots, stage_rows, width), BF16)]
        + [pltpu.VMEM((n, side, m), t) for n, m, t in ((4, side, BF16), (4, side, BF16), (4, 128, F32), (4, 128, F32), (2, side, BF16))]
        + [pltpu.VMEM(w_in.shape, BF16), pltpu.VMEM(w_out.shape, BF16)]
        + [pltpu.VMEM((1, n), F32) for n in lengths]
        + [pltpu.VMEM(acc[name], F32) for name in ACC]
        + [pltpu.VMEM(*scr[name]) for name in SCR]
        + [pltpu.VMEM((room, n), BF16) for n in (width, width, half, wide)]
        + [pltpu.VMEM((width, columns // 2), BF16)]
        + [pltpu.VMEM((size, columns // 2), BF16) for size in room_for]
        + [pltpu.SemaphoreType.DMA((fan, 2 * depth + 2, len(pieces)))] * 2
        + [pltpu.SemaphoreType.DMA((groups, slots))] * 4
        + [pltpu.SemaphoreType.DMA((2, slots)), pltpu.SemaphoreType.DMA((2,))],
        compiler_params=pltpu.CompilerParams(
            collective_id=1, has_side_effects=True, vmem_limit_bytes=64 * 1024 * 1024 - 65536
        ),
        name="layer",
    )(cls, *packed, w_in, w_out, w_pad, vectors)


def local(images, cotangent, res_class, skip, ln_gain, ln_bias, w_in, b_in, gate_gain, gate_bias, w_spatial, b_spatial, w_out, b_out):
    groups = lax.axis_size("patch")
    dp = lax.axis_size("dp")
    count, slot_count, width = images.shape
    half = w_out.shape[0]
    wide = w_in.shape[1]
    slots = count // groups
    quarter = tuple(side * side // groups for side in SIDES)
    patches = groups * slot_count
    side = up(patches, 16)
    span = up(patches, 128)
    stage_rows = up(2 * slot_count, 16)
    me = lax.axis_index("patch").astype(jnp.int32)

    key = jnp.where(skip != 0, res_class + 1, 0).astype(jnp.int32)
    index = jnp.arange(count, dtype=jnp.int32)
    before = (key[None, :] > key[:, None]) | ((key[None, :] == key[:, None]) & (index[None, :] < index[:, None]))
    rank = jnp.sum(before.astype(jnp.int32), axis=1)
    hit = rank[None, :] == index[:, None]
    order = jnp.sum(jnp.where(hit, index[None, :], 0), axis=1)
    slot_index = jnp.arange(slots, dtype=jnp.int32)
    spot = slot_index * groups + jnp.where(slot_index % 2 == 0, me, groups - 1 - me)
    cls = jnp.sum(jnp.where(spot[:, None] == rank[None, :], key[None, :], 0), axis=1)
    me1 = me.reshape(1)

    whole = pl.BlockSpec(memory_space=pltpu.VMEM)
    smem = pl.BlockSpec(memory_space=pltpu.SMEM)
    img_t = jnp.swapaxes(images, 0, 1)
    cot_t = jnp.swapaxes(cotangent, 0, 1)
    planes = (width // 128, slot_count * count, 128)
    packed = pl.pallas_call(
        functools.partial(pack_kernel, slot_count, groups),
        out_shape=[jax.ShapeDtypeStruct((slots, stage_rows, width), BF16)] * groups,
        in_specs=[smem, smem, whole, whole],
        out_specs=[pl.BlockSpec(memory_space=pltpu.HBM)] * groups,
        scratch_shapes=[pltpu.VMEM((groups, slots, stage_rows, width), BF16), pltpu.VMEM(planes, F32), pltpu.VMEM(planes, F32)]
        + [pltpu.VMEM((stage_rows, width), F32), pltpu.SemaphoreType.DMA((groups, slots))],
        compiler_params=pltpu.CompilerParams(vmem_limit_bytes=62 * 1024 * 1024),
        name="pack",
    )(me1, order, img_t, cot_t)

    w_pad = jnp.pad(w_spatial, ((0, side - patches),) * 2)
    vectors = (b_in, gate_gain, gate_bias, ln_gain, ln_bias, b_out, b_spatial)
    filled = sum(v.shape[0] for v in vectors)
    table = jnp.concatenate([*vectors, jnp.zeros((up(filled, 8 * width) - filled,), F32)]).reshape(-1, width)
    lengths = tuple(side if v is b_spatial else v.shape[0] for v in vectors)
    summed, backs = call_layer(cls, packed, w_in, w_out, w_pad, table, lengths, dp, groups, slot_count, quarter, PIECES)
    cut = 512
    inner, outer = wide // cut, half // cut
    far = pl.BlockSpec(memory_space=pl.ANY)
    rowed = [jax.ShapeDtypeStruct((n,), F32) for n in (half, half, width, width, width, wide)]
    swapped = (slot_count, count, width)
    results = pl.pallas_call(
        functools.partial(finish_kernel, slot_count, quarter, wide, half),
        out_shape=[
            jax.ShapeDtypeStruct((width, wide), F32), jax.ShapeDtypeStruct((half, width), F32),
            jax.ShapeDtypeStruct((patches, patches), F32), jax.ShapeDtypeStruct((patches,), F32),
            *rowed, jax.ShapeDtypeStruct(swapped, BF16), jax.ShapeDtypeStruct(swapped, F32),
        ],
        grid=(1 + inner + outer,),
        in_specs=[smem, smem, far, far, far]
        + [pl.BlockSpec((width, cut), lambda t: (0, jnp.where(t == 0, inner + outer, t - 1)))],
        out_specs=[
            pl.BlockSpec((width, cut), lambda t: (0, jnp.clip(t - 1, 0, inner - 1))),
            pl.BlockSpec((cut, width), lambda t: (jnp.maximum(t - 1 - inner, 0), 0)),
        ]
        + [whole] * 8
        + [far, far],
        scratch_shapes=[pltpu.VMEM(planes, F32), pltpu.VMEM(planes, F32), pltpu.VMEM((stage_rows, width), F32)]
        + [pltpu.VMEM(swapped, BF16), pltpu.VMEM(swapped, F32), pltpu.VMEM(swapped, BF16), pltpu.VMEM(swapped, BF16)]
        + [pltpu.VMEM(backs.shape, BF16), pltpu.SemaphoreType.DMA((5,))],
        compiler_params=pltpu.CompilerParams(vmem_limit_bytes=56 * 1024 * 1024),
        name="finish",
    )(rank, key, img_t, cot_t, backs, summed)
    g_w_in, g_w_out, g_w_sp, g_b_sp, g_gate_gain, g_gate_bias, g_ln_gain, g_ln_bias, g_b_out, g_b_in, out_t, grad_t = results
    return (
        jnp.swapaxes(out_t, 0, 1), jnp.swapaxes(grad_t, 0, 1), g_ln_gain, g_ln_bias, g_w_in, g_b_in,
        g_gate_gain, g_gate_bias, g_w_sp, g_b_sp, g_w_out, g_b_out,
    )


def solution(mesh):
    placed = (P("dp", "patch", None),) * 2 + (P("dp"),) * 2 + (P(),) * 10
    return jax.shard_map(
        local, mesh=mesh, in_specs=placed, out_specs=(P("dp", "patch", None),) * 2 + (P(),) * 10, check_vma=False,
    )
```

```python
import functools

import jax
import jax.numpy as jnp
import numpy as np
from jax import lax
from jax.experimental import pallas as pl
from jax.experimental.pallas import tpu as pltpu
from jax.sharding import PartitionSpec as P

MESH = pl.DeviceIdType.MESH
SIDES = (10, 14, 18)
EPS = 1e-05
F32 = jnp.float32
BF16 = jnp.bfloat16
CT = 256
BACKS = (4, 4, 4, 5)
PAIR = 3
PIECES = (("c", 1), ("d", 2), ("b", 2)) * 3 + (("c", 1), ("d", 1), ("b", 1), ("d", 1), ("b", 1))
KEEP = np.float32(1.0) / np.float32(0.9)
GELU_C = np.float32(np.sqrt(2.0 / np.pi))
GELU_K = np.float32(0.044715)


def up(value, unit):
    return -(-value // unit) * unit


def dot(a, b):
    return lax.dot_general(a, b, (((1,), (0,)), ((), ())), preferred_element_type=F32)


def dot_nt(a, b):
    return lax.dot_general(a, b, (((1,), (1,)), ((), ())), preferred_element_type=F32)


def dot_tn(a, b):
    return lax.dot_general(a, b, (((0,), (0,)), ((), ())), preferred_element_type=F32)


def gelu_both(z):
    z2 = z * z
    t = jnp.tanh(z * (GELU_C + (GELU_C * GELU_K) * z2))
    a = 0.5 + 0.5 * t
    g = z * a
    slope = a + (g * (1.0 - t)) * (GELU_C + (3.0 * GELU_C * GELU_K) * z2)
    return g, slope


def fold(v):
    total = v[:, :128]
    for i in range(1, v.shape[1] // 128):
        total = total + v[:, i * 128 : (i + 1) * 128]
    return total


def col8(v):
    return jnp.sum(v.reshape(v.shape[0] // 8, 8, v.shape[1]), axis=0)


def pack_kernel(slot_count, groups, me_ref, order_ref, img_ref, cot_ref, *refs):
    outs, (hold, xf, yf, stage, sem) = refs[:-5], refs[-5:]
    me = me_ref[0]
    count = img_ref.shape[1]
    lanes = xf.shape[0]

    @pl.loop(0, slot_count, unroll=9)
    def _(r):
        at = pl.ds(pl.multiple_of(r * count, 8), count)
        for c in range(lanes):
            xf[c, at, :] = img_ref[r, :, c * 128 : (c + 1) * 128].astype(F32)
            yf[c, at, :] = cot_ref[r, :, c * 128 : (c + 1) * 128].astype(F32)

    @pl.loop(0, outs[0].shape[0])
    def _(j):
        for k in range(groups):
            dest = me ^ k
            which = order_ref[j * groups + jnp.where(lax.rem(j, 2) == 0, dest, groups - 1 - dest)]
            for c in range(lanes):
                cols = slice(c * 128, (c + 1) * 128)
                stage[0:slot_count, cols] = xf[c, pl.ds(which, slot_count, stride=count), :]
                stage[slot_count : 2 * slot_count, cols] = yf[c, pl.ds(which, slot_count, stride=count), :]
            hold[k, j] = stage[...].astype(BF16)
            pltpu.make_async_copy(hold.at[k, j], outs[k].at[j], sem.at[k, j]).start()

    @pl.loop(0, outs[0].shape[0])
    def _(j):
        for k in range(groups):
            pltpu.make_async_copy(hold.at[k, j], outs[k].at[j], sem.at[k, j]).wait()


def finish_kernel(slot_count, quarter, wide, half, rank_ref, key_ref, img_far, cot_far, back_far, src_ref, *refs):
    in_ref, out_w_ref, w_sp_ref, b_sp_ref, *refs = refs
    lines, (out_ref, grad_ref, xf, yf, stage, out, grad, img_ref, cot_ref, back_ref, sem) = refs[:-11], refs[-11:]
    lanes = xf.shape[0]
    count = img_ref.shape[1]
    width, cut = src_ref.shape
    t = pl.program_id(0)
    small, first = 0, 1
    last = first + (wide + half) // cut
    part = -(-count // 3)
    copies = [pltpu.make_async_copy(out, out_ref, sem.at[0]), pltpu.make_async_copy(grad, grad_ref, sem.at[1])]
    loads = [
        pltpu.make_async_copy(a, b, sem.at[2 + i])
        for i, (a, b) in enumerate(((img_far, img_ref), (cot_far, cot_ref), (back_far, back_ref)))
    ]

    @pl.when(t == small)
    def _():
        for load in loads:
            load.start()
        block = src_ref[...].astype(F32)
        patches = w_sp_ref.shape[0]
        side = up(patches, 16)
        w_sp_ref[...] = block[:patches, :patches]
        low = (side - 1) // 128 * 128
        b_sp_ref[...] = block[:side, low : low + 128].T[side - 1 - low, :patches]
        at = side
        for ref in lines:
            for n in range(ref.shape[0] // width):
                ref[n * width : (n + 1) * width] = block[at, :]
                at += 1

    @pl.when(t == first + 1)
    def _():
        for load in loads:
            load.wait()

        @pl.loop(0, slot_count, unroll=9)
        def _(r):
            at = pl.ds(pl.multiple_of(r * count, 8), count)
            for c in range(lanes):
                xf[c, at, :] = img_ref[r, :, c * 128 : (c + 1) * 128].astype(F32)
                yf[c, at, :] = cot_ref[r, :, c * 128 : (c + 1) * 128].astype(F32)

    @pl.when((t >= first) & (t < first + wide // cut))
    def _():
        in_ref[...] = src_ref[...].astype(F32)

    @pl.when(t >= first + wide // cut)
    def _():
        out_w_ref[...] = src_ref[...].astype(F32).T

    @pl.loop(jnp.clip((t - 3) * part, 0, count), jnp.clip((t - 2) * part, 0, count))
    def _(i):
        key = key_ref[i]
        for c, q in enumerate(quarter):

            @pl.when(key == c + 1)
            def _(q=q):
                stage[...] = back_ref[rank_ref[i]].astype(F32)
                at = pl.ds(i, q, stride=count)
                for b in range(lanes):
                    cols = slice(b * 128, (b + 1) * 128)
                    xf[b, at, :] = xf[b, at, :] + stage[0:q, cols]
                    yf[b, at, :] = yf[b, at, :] + stage[slot_count : slot_count + q, cols]

    @pl.when(t == first + 5)
    def _():
        @pl.loop(0, slot_count, unroll=9)
        def _(r):
            at = pl.ds(pl.multiple_of(r * count, 8), count)
            for c in range(lanes):
                out[r, :, c * 128 : (c + 1) * 128] = xf[c, at, :].astype(BF16)
                grad[r, :, c * 128 : (c + 1) * 128] = yf[c, at, :]

        for copy in copies:
            copy.start()

    @pl.when(t == last - 1)
    def _():
        for copy in copies:
            copy.wait()


def image_work(kind, slot, slot_count, me, parcel, par, acc, scr):
    groups = parcel.shape[0]
    rows = scr["xs"].shape[0]
    width = scr["xs"].shape[1]
    half = scr["gate"].shape[1]
    tiles = half // CT
    xs, dys, stage, act, dbr = scr["xs"], scr["dys"], scr["stage"], scr["act"], scr["dbr"]
    vs, gvp, gate, gated, dsp, dgs, dpre = (
        scr["vs"], scr["gvp"], scr["gate"], scr["gated"], scr["dsp"], scr["dgs"], scr["dpre"],
    )
    for m in range(groups):

        @pl.when(me == m)
        def _(m=m):
            for k in range(groups):
                at = (m ^ k) * slot_count
                stage[...] = parcel.at[k, slot][...].astype(F32)
                xs[at : at + slot_count, :] = stage[0:slot_count, :]
                dys[at : at + slot_count, :] = stage[slot_count : 2 * slot_count, :]

    x = xs[0:rows, :]
    mean = jnp.mean(x, axis=-1, keepdims=True)
    cen = x - mean
    inv = lax.rsqrt(jnp.mean(cen * cen, axis=-1, keepdims=True) + EPS)
    xhat = cen * inv
    xs[0:rows, :] = xhat
    scr["inv"][0:rows, :] = jnp.broadcast_to(inv, (rows, 128))
    act[0:rows, :] = (xhat * par["ln_gain"][...] + par["ln_bias"][...]).astype(BF16)
    db = (dys[0:rows, :] * par["live"][kind, :, 0:1]).astype(BF16)
    dbr[0:rows, :] = db
    acc["b_out"][...] += col8(db.astype(F32))

    @pl.loop(0, tiles, unroll=tiles)
    def _(t):
        at = pl.ds(pl.multiple_of(t * CT, CT), CT)
        far = pl.ds(pl.multiple_of(half + t * CT, CT), CT)
        z = dot(act[0:rows, :], par["w_in"][:, far]) + par["b_in"][:, far]
        g, slope = gelu_both(z)
        vs[0:rows, at] = g
        gvp[0:rows, at] = slope.astype(BF16)

    total = fold(vs[0:rows, :])
    vmean = jnp.sum(total, axis=-1, keepdims=True) / half
    cen = vs[0:rows, :] - vmean
    vinv = lax.rsqrt(jnp.sum(fold(cen * cen), axis=-1, keepdims=True) / half + EPS)
    vhat = cen * vinv
    vs[0:rows, :] = vhat
    gate[0:rows, :] = (vhat * par["gate_gain"][...] + par["gate_bias"][...]).astype(BF16)
    last = lax.broadcasted_iota(jnp.int32, (16, 1), 0) == 15
    gate[rows - 16 : rows, :] = jnp.where(last, 1.0, gate[rows - 16 : rows, :].astype(F32)).astype(BF16)
    scr["hs"][0:rows, :] = jnp.zeros((rows, 128), F32)
    scr["hv"][0:rows, :] = jnp.zeros((rows, 128), F32)

    @pl.loop(0, tiles, unroll=tiles)
    def _(t):
        at = pl.ds(pl.multiple_of(t * CT, CT), CT)
        z = dot(act[0:rows, :], par["w_in"][:, at]) + par["b_in"][:, at]
        u, slope = gelu_both(z)
        sp = dot(par["wsp"][kind], gate[0:rows, at]) + par["bsp"][kind, :, 0:1]
        gated[0:rows, at] = (u * sp).astype(BF16)
        dg = dot_nt(dbr[0:rows, :], par["w_out"][at, :])
        pre = (dg * sp * slope).astype(BF16)
        dpre[0:rows, at] = pre
        ds = (dg * u).astype(BF16)
        dsp[0:rows, at] = ds
        dgate = dot(par["wsp_t"][kind], ds)
        vh = vs[0:rows, at]
        acc["gate_bias"][:, at] += col8(dgate)
        acc["gate_gain"][:, at] += col8(dgate * vh)
        h = dgate * par["gate_gain"][:, at]
        dgs[0:rows, at] = h
        scr["hs"][0:rows, :] += fold(h)
        scr["hv"][0:rows, :] += fold(h * vh)

    hmean = jnp.sum(scr["hs"][0:rows, :], axis=-1, keepdims=True) / half
    hvmean = jnp.sum(scr["hv"][0:rows, :], axis=-1, keepdims=True) / half

    @pl.loop(0, tiles, unroll=tiles)
    def _(t):
        at = pl.ds(pl.multiple_of(t * CT, CT), CT)
        far = pl.ds(pl.multiple_of(half + t * CT, CT), CT)
        dv = vinv * (dgs[0:rows, at] - hmean - vs[0:rows, at] * hvmean)
        pre = (dv * gvp[0:rows, at].astype(F32)).astype(BF16)
        dpre[0:rows, far] = pre

    mixed = dot_nt(dsp[0:rows, :], gate[0:rows, :])
    for c in range(acc["w_sp"].shape[0]):
        acc["w_sp"][c, :, 0:rows] += jnp.where(kind == c + 1, mixed, 0.0)
    branch = dot(gated[0:rows, :], par["w_out"][...]) + par["b_out"][...]
    dys[0:rows, :] = branch * KEEP
    dact = dot_nt(dpre[0:rows, :], par["w_in"][...])
    xhat = xs[0:rows, :]
    acc["ln_bias"][...] += col8(dact)
    acc["ln_gain"][...] += col8(dact * xhat)
    h = dact * par["ln_gain"][...]
    back = scr["inv"][0:rows, 0:1] * (
        h - jnp.mean(h, axis=-1, keepdims=True) - xhat * jnp.mean(h * xhat, axis=-1, keepdims=True)
    )
    xs[0:rows, :] = back
    for m in range(groups):

        @pl.when(me == m)
        def _(m=m):
            for k in range(groups):
                at = (m ^ k) * slot_count
                stage[0:slot_count, :] = dys[at : at + slot_count, :]
                stage[slot_count : 2 * slot_count, :] = xs[at : at + slot_count, :]
                parcel[k, slot] = stage[...].astype(BF16)


VECTORS = ("b_in", "gate_gain", "gate_bias", "ln_gain", "ln_bias", "b_out", "b_sp")
LARGE = ("w_in", "w_out")
TABLES = ("wsp", "wsp_t", "bsp", "live", "pick")
ACC = ("w_sp", "gate_gain", "gate_bias", "ln_gain", "ln_bias", "b_out", "w_in", "w_out")
SCR = ("stage", "xs", "dys", "inv", "vs", "gvp", "gate", "dsp", "dgs", "hs", "hv")
KEPT = ("act", "dbr", "gated", "dpre")


def reduce_orders(dp):
    bits = [1 << b for b in range(dp.bit_length() - 1)]
    x, z, y = [("dp", bits[:1])], [("dp", [bit]) for bit in bits[1:3]], [("patch", [2])]
    rest = [("dp", [bit]) for bit in bits[3:]]
    return {
        "a": x + y + z + rest, "b": y + x + z + rest, "c": z + x + y + rest, "d": x + z + y + rest, "e": y + z + x + rest,
    }


def combos(bits):
    masks = [0]
    for bit in bits:
        masks += [mask | bit for mask in masks]
    return masks[1:]


def plan_sizes(order, rows):
    sizes = [rows]
    for _, bits in order:
        keep = sizes[-1] >> len(bits)
        sizes.append(keep if keep >= 16 else sizes[-1])
    return sizes


LINES = ("gate_gain", "gate_bias", "ln_gain", "ln_bias", "b_out")


def fill_tables(par, quarter, slot_count, groups):
    side = par["wsp"].shape[1]
    t = lax.broadcasted_iota(jnp.int32, (side, 1), 0)
    lane = lax.broadcasted_iota(jnp.int32, (1, slot_count * groups), 1)
    lanes = lax.broadcasted_iota(jnp.int32, (1, side), 1)
    place = sum(jnp.where(t >= slot_count * g, 1, 0) for g in range(1, groups))
    within = t - slot_count * place
    w = par["w_sp"][...]
    for name in ("wsp", "wsp_t", "bsp", "live"):
        par[name][0] = jnp.zeros(par[name].shape[1:], par[name].dtype)
    for c, q in enumerate(quarter):
        live = (within < q) & (t < slot_count * groups)
        hit = live & (place * q + within == lane)
        low = jnp.where(hit, 1.0, 0.0).astype(BF16)
        par["wsp"][c + 1] = dot_nt(dot(low, w).astype(BF16), low).astype(BF16)
        par["wsp_t"][c + 1] = dot_nt(dot_nt(low, w).astype(BF16), low).astype(BF16)
        bias = jnp.sum(jnp.where(hit, par["b_sp"][...], 0.0), axis=-1, keepdims=True)
        par["bsp"][c + 1] = jnp.broadcast_to(bias, (side, 128))
        par["live"][c + 1] = jnp.broadcast_to(jnp.where(live, KEEP, 0.0), (side, 128))
        if c < 2:
            corner = (t == side - 1) & (lanes == side - 1)
            chosen = (live & (place * q + within == lanes)) | corner
            par["pick"][c] = jnp.where(chosen, 1.0, 0.0).astype(BF16)


def gather_gradients(total_ref, par, acc, kept):
    act_t = jnp.concatenate([kept["act"][...].T, jnp.ones((16, kept["act"].shape[0]), BF16)], axis=0)
    for t in range(acc["w_in"].shape[1] // CT):
        at = slice(t * CT, (t + 1) * CT)
        acc["w_in"][:, at] += dot(act_t, kept["dpre"][:, at])
    dbr_t = kept["dbr"][...].T
    for t in range(acc["w_out"].shape[1] // CT):
        at = slice(t * CT, (t + 1) * CT)
        acc["w_out"][:, at] += dot(dbr_t, kept["gated"][:, at])


def lay_out(total_ref, par, acc):
    width, half = acc["w_out"].shape
    wide = acc["w_in"].shape[1]
    base = wide + half
    rows, span = acc["w_sp"].shape[1:]
    total_ref[:, 0:wide] = acc["w_in"][0:width, :].astype(BF16)
    total_ref[:, wide:base] = acc["w_out"][...].astype(BF16)
    mix = acc["w_sp"][2, :, 0:rows]
    for c in range(2):
        pick = par["pick"][c]
        part = dot(acc["w_sp"][c, :, 0:rows].astype(BF16), pick).astype(BF16)
        mix = mix + dot_tn(pick, part)
    total_ref[:, base:] = jnp.zeros((width, total_ref.shape[1] - base), BF16)
    total_ref[0:rows, base : base + rows] = mix.astype(BF16)
    lines = []
    for name in LINES:
        v = jnp.sum(acc[name][...], axis=0, keepdims=True)
        lines += [v[:, i * width : (i + 1) * width] for i in range(v.shape[1] // width)]
    more = [acc["w_in"][width : width + 1, i * width : (i + 1) * width] for i in range(wide // width)]
    more.append(jnp.zeros((32 - len(lines) - len(more), width), F32))
    total_ref[rows : rows + 32, base : base + width] = jnp.concatenate(lines + more, axis=0).astype(BF16)


def layer_kernel(orders, spans, sizes, slot_count, groups, quarter, pair, cls_ref, *refs):
    depth = len(orders[0])
    packed, refs = refs[:groups], refs[groups:]
    weights, w_sp_ref, given, refs = refs[:2], refs[2], refs[3 : 3 + len(VECTORS)], refs[3 + len(VECTORS) :]
    out_ref, back_ref, total_ref, parcel, *refs = refs
    names = TABLES + LARGE + VECTORS
    par, refs = {"w_sp": w_sp_ref} | dict(zip(names, refs)), refs[len(names) :]
    acc, refs = dict(zip(ACC, refs)), refs[len(ACC) :]
    scr, refs = dict(zip(SCR, refs)), refs[len(SCR) :]
    kept, refs = dict(zip(KEPT, refs)), refs[len(KEPT) :]
    first, *refs = refs
    rbufs, refs = refs[:depth], refs[depth:]
    send_sem, recv_sem, in_send, in_recv, back_send, back_recv, own_sem, load_sem = refs
    dp, patch = lax.axis_index("dp"), lax.axis_index("patch")
    core = patch & 1

    def peer(axis, bit):
        return (dp ^ bit, patch) if axis == "dp" else (dp, patch ^ bit)

    peers = [peer("patch", 1), peer("patch", 3)] + [peer(a, mask) for a, bits in orders[0] for mask in combos(bits)]
    barrier = pltpu.get_barrier_semaphore()
    for other in peers:
        pl.semaphore_signal(barrier, inc=1, device_id=other, device_id_type=MESH)
    pl.semaphore_wait(barrier, len(peers))

    slots = parcel.shape[1]

    def inward(k, j):
        if k == 0:
            return pltpu.make_async_copy(packed[0].at[j], parcel.at[0, j], own_sem.at[0, j])
        return pltpu.make_async_remote_copy(
            src_ref=packed[k].at[j], dst_ref=parcel.at[k, j], send_sem=in_send.at[k, j], recv_sem=in_recv.at[k, j],
            device_id=peer("patch", k), device_id_type=MESH,
        )

    def back(k, j):
        place = j * groups + jnp.where(lax.rem(j, 2) == 0, patch, groups - 1 - patch)
        if k == 0:
            return pltpu.make_async_copy(parcel.at[0, j], back_ref.at[place], own_sem.at[1, j])
        return pltpu.make_async_remote_copy(
            src_ref=parcel.at[k, j], dst_ref=back_ref.at[place], send_sem=back_send.at[k, j], recv_sem=back_recv.at[k, j],
            device_id=peer("patch", k), device_id_type=MESH,
        )

    def give_back(begin, end):
        @pl.loop(begin, end)
        def _(j):
            for k in range(groups - 1, -1, -1):
                back(k, j).start()

    stops = [slots * n // 6 for n in (0, *BACKS, 6)]

    @pl.loop(0, slots)
    def _(j):
        for k in range(groups - 1, -1, -1):
            inward(k, j).start()

    loads = [pltpu.make_async_copy(weights[i], par[name], load_sem.at[i]) for i, name in enumerate(LARGE)]
    for load in loads:
        load.start()
    for name, ref in zip(VECTORS, given):
        par[name][...] = ref[...].reshape(1, ref.shape[0])
    fill_tables(par, quarter, slot_count, groups)
    for ref in acc.values():
        ref[...] = jnp.zeros_like(ref)
    rows = scr["xs"].shape[0]
    for ref in kept.values():
        if ref.shape[0] > pair * rows:
            ref[pair * rows :, :] = jnp.zeros((ref.shape[0] - pair * rows, ref.shape[1]), BF16)
    n = groups * slot_count
    for name in ("xs", "dys"):
        scr[name][rows - 16 : rows, :] = jnp.zeros((16, scr[name].shape[1]), F32)
    for load in loads:
        load.wait()

    @pl.loop(0, slots)
    def _(j):
        for k in range(groups):
            inward(k, j).wait()

        @pl.when(j == slots - 2)
        def _():
            give_back(stops[0], stops[1])

        @pl.when(j == slots - 1)
        def _():
            give_back(stops[1], stops[2])

        half_at = pl.ds(pl.multiple_of(lax.rem(j, pair) * rows, 16), rows)
        views = {name: ref.at[half_at] for name, ref in kept.items()}
        image_work(cls_ref[j], j, slot_count, patch, parcel, par, acc, scr | views)

        @pl.when(lax.rem(j, pair) == pair - 1)
        def _():
            gather_gradients(total_ref, par, acc, kept)

    lay_out(total_ref, par, acc)
    half = total_ref.shape[1] // 2
    tall = total_ref.shape[0]
    pieces = len(orders)
    mine = pl.multiple_of(core * half, 128)
    theirs = pl.multiple_of((1 - core) * half, 128)
    copies = []

    def send(src, dst, step, i, part, other):
        copy = pltpu.make_async_remote_copy(
            src_ref=src, dst_ref=dst, send_sem=send_sem.at[part, step, i], recv_sem=recv_sem.at[part, step, i], device_id=other,
            device_id_type=MESH,
        )
        copy.start()
        copies.append(copy)
        return copy

    def cols(i):
        return pl.ds(spans[i][0], spans[i][1])

    def shifted(base, i):
        return pl.ds(pl.multiple_of(base + spans[i][0], 128), spans[i][1])

    def rank_in(axis, bits):
        index = dp if axis == "dp" else patch
        return sum(jnp.where((index & bit) != 0, 1 << n, 0) for n, bit in enumerate(bits))

    def other_rank(axis, bits, mask):
        index = (dp if axis == "dp" else patch) ^ mask
        return sum(jnp.where((index & bit) != 0, 1 << n, 0) for n, bit in enumerate(bits))

    def rows_at(begin, size):
        return pl.ds(pl.multiple_of(begin, 16), size)

    state = [0] * pieces
    flying = [
        [send(total_ref.at[:, shifted(theirs, i)], first.at[:, cols(i)], 0, i, 0, peer("patch", 1))] for i in range(pieces)
    ]
    give_back(stops[2], stops[3])
    for s in range(depth + 1):
        if s == 2:
            give_back(stops[3], stops[4])
        for i in range(pieces):
            size = sizes[i][s]
            for copy in flying[i]:
                copy.wait_recv()
            lo = state[i]
            if s > 0 and sizes[i][s - 1] == size:
                for copy in flying[i]:
                    copy.wait_send()
                copies[:] = [copy for copy in copies if all(copy is not old for old in flying[i])]
            got_ref = first if s == 0 else rbufs[s - 1]
            unit = 32 if size % 32 == 0 else 16

            @pl.loop(0, size, step=unit)
            def _(r, i=i, lo=lo, got_ref=got_ref, unit=unit, size=size, parts=len(flying[i])):
                at = rows_at(lo + r, unit)
                value = total_ref[at, shifted(mine, i)].astype(F32)
                for part in range(parts):
                    value = value + got_ref[rows_at(part * size + r, unit), cols(i)].astype(F32)
                total_ref[at, shifted(mine, i)] = value.astype(BF16)

            if s < depth:
                axis, bits = orders[i][s]
                keep = sizes[i][s + 1]
                base = state[i]
                split = keep < size
                if split:
                    state[i] = base + rank_in(axis, bits) * keep
                flying[i] = []
                for part, mask in enumerate(combos(bits)):
                    give = base + other_rank(axis, bits, mask) * keep if split else base
                    flying[i].append(
                        send(
                            total_ref.at[rows_at(give, keep), shifted(mine, i)],
                            rbufs[s].at[pl.ds(part * keep, keep), cols(i)], s + 1, i, part, peer(axis, mask),
                        )
                    )
    for i in range(pieces):
        at = rows_at(state[i], sizes[i][depth])
        out_ref[at, shifted(mine, i)] = total_ref[at, shifted(mine, i)]
    flying = [[] for _ in range(pieces)]
    for s in range(depth, -1, -1):
        if s == depth - 1:
            give_back(stops[4], stops[5])
        for i in range(pieces):
            for copy in flying[i]:
                copy.wait_recv()
            flying[i] = []
            step = 2 * depth + 1 - s
            if s == 0:
                where = out_ref.at[:, shifted(mine, i)]
                flying[i] = [send(where, where, step, i, 0, peer("patch", 1))]
            elif sizes[i][s] < sizes[i][s - 1]:
                axis, bits = orders[i][s - 1]
                where = out_ref.at[rows_at(state[i], sizes[i][s]), shifted(mine, i)]
                for part, mask in enumerate(combos(bits)):
                    flying[i].append(send(where, where, step, i, part, peer(axis, mask)))
                state[i] = state[i] - rank_in(axis, bits) * sizes[i][s]
    for i in range(pieces):
        for copy in flying[i]:
            copy.wait_recv()

    @pl.loop(0, slots)
    def _(j):
        for k in range(groups):
            back(k, j).wait()

    for copy in copies:
        copy.wait_send()


def call_layer(cls, packed, w_in, w_out, w_spatial, vectors, dp, groups, slot_count, quarter, pieces):
    slots, stage_rows, width = packed[0].shape
    wide, half, side = w_in.shape[1], w_out.shape[0], up(w_spatial.shape[0], 16)
    span = up(side, 128)
    pair = PAIR if slots % PAIR == 0 else 1
    columns = wide + half + width
    table = reduce_orders(dp)
    orders = [table[name] for name, _ in pieces]
    starts = np.cumsum([0] + [w * 128 for _, w in pieces])
    spans = [(int(starts[i]), w * 128) for i, (_, w) in enumerate(pieces)]
    depth = len(orders[0])
    sizes = [plan_sizes(order, width) for order in orders]
    room_for = [
        max(len(combos(order[s][1])) * size[s + 1] for order, size in zip(orders, sizes)) for s in range(depth)
    ]
    fan = max(len(combos(bits)) for _, bits in orders[0])
    vmem = pl.BlockSpec(memory_space=pltpu.VMEM)
    far = pl.BlockSpec(memory_space=pl.ANY)
    acc = {
        "w_sp": (3, side, span), "gate_gain": (8, half), "gate_bias": (8, half), "ln_gain": (8, width),
        "ln_bias": (8, width), "b_out": (8, width), "w_in": (width + 16, wide), "w_out": (width, half),
    }
    scr = {
        "stage": ((stage_rows, width), F32), "xs": ((side, width), F32), "dys": ((side, width), F32),
        "inv": ((side, 128), F32), "vs": ((side, half), F32), "gvp": ((side, half), BF16), "gate": ((side, half), BF16),
        "dsp": ((side, half), BF16), "dgs": ((side, half), F32), "hs": ((side, 128), F32), "hv": ((side, 128), F32),
    }
    room = up(pair * side, 256)
    return pl.pallas_call(
        functools.partial(layer_kernel, orders, spans, sizes, slot_count, groups, quarter, pair),
        out_shape=[
            jax.ShapeDtypeStruct((width, columns), BF16),
            jax.ShapeDtypeStruct((slots * groups, stage_rows, width), BF16),
        ],
        in_specs=[pl.BlockSpec(memory_space=pltpu.SMEM)] + [far] * groups + [far, far, vmem] + [vmem] * len(vectors),
        out_specs=[vmem, far],
        scratch_shapes=[pltpu.VMEM((width, columns), BF16), pltpu.VMEM((groups, slots, stage_rows, width), BF16)]
        + [pltpu.VMEM((n, side, m), t) for n, m, t in ((4, side, BF16), (4, side, BF16), (4, 128, F32), (4, 128, F32), (2, side, BF16))]
        + [pltpu.VMEM(w_in.shape, BF16), pltpu.VMEM(w_out.shape, BF16)]
        + [pltpu.VMEM((1, v.shape[0]), F32) for v in vectors]
        + [pltpu.VMEM(acc[name], F32) for name in ACC]
        + [pltpu.VMEM(*scr[name]) for name in SCR]
        + [pltpu.VMEM((room, n), BF16) for n in (width, width, half, wide)]
        + [pltpu.VMEM((width, columns // 2), BF16)]
        + [pltpu.VMEM((size, columns // 2), BF16) for size in room_for]
        + [pltpu.SemaphoreType.DMA((fan, 2 * depth + 2, len(pieces)))] * 2
        + [pltpu.SemaphoreType.DMA((groups, slots))] * 4
        + [pltpu.SemaphoreType.DMA((2, slots)), pltpu.SemaphoreType.DMA((2,))],
        compiler_params=pltpu.CompilerParams(
            collective_id=1, has_side_effects=True, vmem_limit_bytes=64 * 1024 * 1024 - 65536
        ),
        name="layer",
    )(cls, *packed, w_in, w_out, w_spatial, *vectors)


def local(images, cotangent, res_class, skip, ln_gain, ln_bias, w_in, b_in, gate_gain, gate_bias, w_spatial, b_spatial, w_out, b_out):
    groups = lax.axis_size("patch")
    dp = lax.axis_size("dp")
    count, slot_count, width = images.shape
    half = w_out.shape[0]
    wide = w_in.shape[1]
    slots = count // groups
    quarter = tuple(side * side // groups for side in SIDES)
    patches = groups * slot_count
    side = up(patches, 16)
    stage_rows = up(2 * slot_count, 16)
    me = lax.axis_index("patch").astype(jnp.int32)

    key = jnp.where(skip != 0, res_class + 1, 0).astype(jnp.int32)
    index = jnp.arange(count, dtype=jnp.int32)
    before = (key[None, :] > key[:, None]) | ((key[None, :] == key[:, None]) & (index[None, :] < index[:, None]))
    rank = jnp.sum(before.astype(jnp.int32), axis=1)
    hit = rank[None, :] == index[:, None]
    order = jnp.sum(jnp.where(hit, index[None, :], 0), axis=1)
    slot_index = jnp.arange(slots, dtype=jnp.int32)
    spot = slot_index * groups + jnp.where(slot_index % 2 == 0, me, groups - 1 - me)
    cls = jnp.sum(jnp.where(spot[:, None] == rank[None, :], key[None, :], 0), axis=1)
    me1 = me.reshape(1)

    whole = pl.BlockSpec(memory_space=pltpu.VMEM)
    smem = pl.BlockSpec(memory_space=pltpu.SMEM)
    img_t = jnp.swapaxes(images, 0, 1)
    cot_t = jnp.swapaxes(cotangent, 0, 1)
    planes = (width // 128, slot_count * count, 128)
    packed = pl.pallas_call(
        functools.partial(pack_kernel, slot_count, groups),
        out_shape=[jax.ShapeDtypeStruct((slots, stage_rows, width), BF16)] * groups,
        in_specs=[smem, smem, whole, whole],
        out_specs=[pl.BlockSpec(memory_space=pltpu.HBM)] * groups,
        scratch_shapes=[pltpu.VMEM((groups, slots, stage_rows, width), BF16), pltpu.VMEM(planes, F32), pltpu.VMEM(planes, F32)]
        + [pltpu.VMEM((stage_rows, width), F32), pltpu.SemaphoreType.DMA((groups, slots))],
        compiler_params=pltpu.CompilerParams(vmem_limit_bytes=62 * 1024 * 1024),
        name="pack",
    )(me1, order, img_t, cot_t)

    vectors = (b_in, gate_gain, gate_bias, ln_gain, ln_bias, b_out, b_spatial)
    summed, backs = call_layer(cls, packed, w_in, w_out, w_spatial, vectors, dp, groups, slot_count, quarter, PIECES)
    cut = 512
    inner, outer = wide // cut, half // cut
    far = pl.BlockSpec(memory_space=pl.ANY)
    rowed = [jax.ShapeDtypeStruct((n,), F32) for n in (half, half, width, width, width, wide)]
    swapped = (slot_count, count, width)
    results = pl.pallas_call(
        functools.partial(finish_kernel, slot_count, quarter, wide, half),
        out_shape=[
            jax.ShapeDtypeStruct((width, wide), F32), jax.ShapeDtypeStruct((half, width), F32),
            jax.ShapeDtypeStruct((patches, patches), F32), jax.ShapeDtypeStruct((patches,), F32),
            *rowed, jax.ShapeDtypeStruct(swapped, BF16), jax.ShapeDtypeStruct(swapped, F32),
        ],
        grid=(1 + inner + outer,),
        in_specs=[smem, smem, far, far, far]
        + [pl.BlockSpec((width, cut), lambda t: (0, jnp.where(t == 0, inner + outer, t - 1)))],
        out_specs=[
            pl.BlockSpec((width, cut), lambda t: (0, jnp.clip(t - 1, 0, inner - 1))),
            pl.BlockSpec((cut, width), lambda t: (jnp.maximum(t - 1 - inner, 0), 0)),
        ]
        + [whole] * 8
        + [far, far],
        scratch_shapes=[pltpu.VMEM(planes, F32), pltpu.VMEM(planes, F32), pltpu.VMEM((stage_rows, width), F32)]
        + [pltpu.VMEM(swapped, BF16), pltpu.VMEM(swapped, F32), pltpu.VMEM(swapped, BF16), pltpu.VMEM(swapped, BF16)]
        + [pltpu.VMEM(backs.shape, BF16), pltpu.SemaphoreType.DMA((5,))],
        compiler_params=pltpu.CompilerParams(vmem_limit_bytes=56 * 1024 * 1024),
        name="finish",
    )(rank, key, img_t, cot_t, backs, summed)
    g_w_in, g_w_out, g_w_sp, g_b_sp, g_gate_gain, g_gate_bias, g_ln_gain, g_ln_bias, g_b_out, g_b_in, out_t, grad_t = results
    return (
        jnp.swapaxes(out_t, 0, 1), jnp.swapaxes(grad_t, 0, 1), g_ln_gain, g_ln_bias, g_w_in, g_b_in,
        g_gate_gain, g_gate_bias, g_w_sp, g_b_sp, g_w_out, g_b_out,
    )


def solution(mesh):
    placed = (P("dp", "patch", None),) * 2 + (P("dp"),) * 2 + (P(),) * 10
    return jax.shard_map(
        local, mesh=mesh, in_specs=placed, out_specs=(P("dp", "patch", None),) * 2 + (P(),) * 10, check_vma=False,
    )
```

```python
import functools

import jax
import jax.numpy as jnp
import numpy as np
from jax import lax
from jax.experimental import pallas as pl
from jax.experimental.pallas import tpu as pltpu
from jax.sharding import PartitionSpec as P

MESH = pl.DeviceIdType.MESH
SIDES = (10, 14, 18)
EPS = 1e-05
F32 = jnp.float32
BF16 = jnp.bfloat16
CT = 256
BACKS = (4, 4, 4, 5)
PAIR = 3
PIECES = (("c", 1), ("d", 2), ("b", 2)) * 3 + (("c", 1), ("d", 1), ("b", 1), ("d", 1), ("b", 1))
KEEP = np.float32(1.0) / np.float32(0.9)
GELU_C = np.float32(np.sqrt(2.0 / np.pi))
GELU_K = np.float32(0.044715)


def up(value, unit):
    return -(-value // unit) * unit


def dot(a, b):
    return lax.dot_general(a, b, (((1,), (0,)), ((), ())), preferred_element_type=F32)


def dot_nt(a, b):
    return lax.dot_general(a, b, (((1,), (1,)), ((), ())), preferred_element_type=F32)


def dot_tn(a, b):
    return lax.dot_general(a, b, (((0,), (0,)), ((), ())), preferred_element_type=F32)


def gelu_both(z):
    z2 = z * z
    t = jnp.tanh(z * (GELU_C + (GELU_C * GELU_K) * z2))
    a = 0.5 + 0.5 * t
    g = z * a
    slope = a + (g * (1.0 - t)) * (GELU_C + (3.0 * GELU_C * GELU_K) * z2)
    return g, slope


def fold(v):
    total = v[:, :128]
    for i in range(1, v.shape[1] // 128):
        total = total + v[:, i * 128 : (i + 1) * 128]
    return total


def col8(v):
    return jnp.sum(v.reshape(v.shape[0] // 8, 8, v.shape[1]), axis=0)


def pack_kernel(slot_count, groups, me_ref, order_ref, img_ref, cot_ref, *refs):
    outs, (hold, xf, yf, stage, sem) = refs[:-5], refs[-5:]
    me = me_ref[0]
    count = img_ref.shape[1]
    lanes = xf.shape[0]

    @pl.loop(0, slot_count, unroll=9)
    def _(r):
        at = pl.ds(pl.multiple_of(r * count, 8), count)
        for c in range(lanes):
            xf[c, at, :] = img_ref[r, :, c * 128 : (c + 1) * 128].astype(F32)
            yf[c, at, :] = cot_ref[r, :, c * 128 : (c + 1) * 128].astype(F32)

    @pl.loop(0, outs[0].shape[0])
    def _(j):
        for k in range(groups):
            dest = me ^ k
            which = order_ref[j * groups + jnp.where(lax.rem(j, 2) == 0, dest, groups - 1 - dest)]
            for c in range(lanes):
                cols = slice(c * 128, (c + 1) * 128)
                stage[0:slot_count, cols] = xf[c, pl.ds(which, slot_count, stride=count), :]
                stage[slot_count : 2 * slot_count, cols] = yf[c, pl.ds(which, slot_count, stride=count), :]
            hold[k, j] = stage[...].astype(BF16)
            pltpu.make_async_copy(hold.at[k, j], outs[k].at[j], sem.at[k, j]).start()

    @pl.loop(0, outs[0].shape[0])
    def _(j):
        for k in range(groups):
            pltpu.make_async_copy(hold.at[k, j], outs[k].at[j], sem.at[k, j]).wait()


def finish_kernel(slot_count, quarter, wide, half, rank_ref, key_ref, img_far, cot_far, back_far, src_ref, *refs):
    in_ref, out_w_ref, w_sp_ref, b_sp_ref, *refs = refs
    lines, (out_ref, grad_ref, xf, yf, stage, out, grad, img_ref, cot_ref, back_ref, sem) = refs[:-11], refs[-11:]
    lanes = xf.shape[0]
    count = img_ref.shape[1]
    width, cut = src_ref.shape
    t = pl.program_id(0)
    small, first = 0, 1
    last = first + (wide + half) // cut
    part = -(-count // 3)
    copies = [pltpu.make_async_copy(out, out_ref, sem.at[0]), pltpu.make_async_copy(grad, grad_ref, sem.at[1])]
    loads = [
        pltpu.make_async_copy(a, b, sem.at[2 + i])
        for i, (a, b) in enumerate(((img_far, img_ref), (cot_far, cot_ref), (back_far, back_ref)))
    ]

    @pl.when(t == small)
    def _():
        for load in loads:
            load.start()
        block = src_ref[...].astype(F32)
        patches = w_sp_ref.shape[0]
        side = up(patches, 16)
        w_sp_ref[...] = block[:patches, :patches]
        low = (side - 1) // 128 * 128
        b_sp_ref[...] = block[:side, low : low + 128].T[side - 1 - low, :patches]
        at = side
        for ref in lines:
            for n in range(ref.shape[0] // width):
                ref[n * width : (n + 1) * width] = block[at, :]
                at += 1

    @pl.when(t == first + 1)
    def _():
        for load in loads:
            load.wait()

        @pl.loop(0, slot_count, unroll=9)
        def _(r):
            at = pl.ds(pl.multiple_of(r * count, 8), count)
            for c in range(lanes):
                xf[c, at, :] = img_ref[r, :, c * 128 : (c + 1) * 128].astype(F32)
                yf[c, at, :] = cot_ref[r, :, c * 128 : (c + 1) * 128].astype(F32)

    @pl.when((t >= first) & (t < first + wide // cut))
    def _():
        in_ref[...] = src_ref[...].astype(F32)

    @pl.when(t >= first + wide // cut)
    def _():
        out_w_ref[...] = src_ref[...].astype(F32).T

    @pl.loop(jnp.clip((t - 3) * part, 0, count), jnp.clip((t - 2) * part, 0, count))
    def _(i):
        key = key_ref[i]
        for c, q in enumerate(quarter):

            @pl.when(key == c + 1)
            def _(q=q):
                stage[...] = back_ref[rank_ref[i]].astype(F32)
                at = pl.ds(i, q, stride=count)
                for b in range(lanes):
                    cols = slice(b * 128, (b + 1) * 128)
                    xf[b, at, :] = xf[b, at, :] + stage[0:q, cols]
                    yf[b, at, :] = yf[b, at, :] + stage[slot_count : slot_count + q, cols]

    @pl.when(t == first + 5)
    def _():
        @pl.loop(0, slot_count, unroll=9)
        def _(r):
            at = pl.ds(pl.multiple_of(r * count, 8), count)
            for c in range(lanes):
                out[r, :, c * 128 : (c + 1) * 128] = xf[c, at, :].astype(BF16)
                grad[r, :, c * 128 : (c + 1) * 128] = yf[c, at, :]

        for copy in copies:
            copy.start()

    @pl.when(t == last - 1)
    def _():
        for copy in copies:
            copy.wait()


def image_work(kind, slot, slot_count, me, parcel, par, acc, scr):
    groups = parcel.shape[0]
    rows = scr["xs"].shape[0]
    width = scr["xs"].shape[1]
    half = scr["gate"].shape[1]
    tiles = half // CT
    xs, dys, stage, act, dbr = scr["xs"], scr["dys"], scr["stage"], scr["act"], scr["dbr"]
    vs, gvp, gate, gated, dsp, dgs, dpre = (
        scr["vs"], scr["gvp"], scr["gate"], scr["gated"], scr["dsp"], scr["dgs"], scr["dpre"],
    )
    for m in range(groups):

        @pl.when(me == m)
        def _(m=m):
            for k in range(groups):
                at = (m ^ k) * slot_count
                stage[...] = parcel.at[k, slot][...].astype(F32)
                xs[at : at + slot_count, :] = stage[0:slot_count, :]
                dys[at : at + slot_count, :] = stage[slot_count : 2 * slot_count, :]

    x = xs[0:rows, :]
    mean = jnp.mean(x, axis=-1, keepdims=True)
    cen = x - mean
    inv = lax.rsqrt(jnp.mean(cen * cen, axis=-1, keepdims=True) + EPS)
    xhat = cen * inv
    xs[0:rows, :] = xhat
    scr["inv"][0:rows, :] = jnp.broadcast_to(inv, (rows, 128))
    act[0:rows, :] = (xhat * par["ln_gain"][...] + par["ln_bias"][...]).astype(BF16)
    db = (dys[0:rows, :] * par["live"][kind, :, 0:1]).astype(BF16)
    dbr[0:rows, :] = db
    acc["b_out"][...] += col8(db.astype(F32))

    @pl.loop(0, tiles, unroll=tiles)
    def _(t):
        at = pl.ds(pl.multiple_of(t * CT, CT), CT)
        far = pl.ds(pl.multiple_of(half + t * CT, CT), CT)
        z = dot(act[0:rows, :], par["w_in"][:, far]) + par["b_in"][:, far]
        g, slope = gelu_both(z)
        vs[0:rows, at] = g
        gvp[0:rows, at] = slope.astype(BF16)

    total = fold(vs[0:rows, :])
    vmean = jnp.sum(total, axis=-1, keepdims=True) / half
    cen = vs[0:rows, :] - vmean
    vinv = lax.rsqrt(jnp.sum(fold(cen * cen), axis=-1, keepdims=True) / half + EPS)
    vhat = cen * vinv
    vs[0:rows, :] = vhat
    gate[0:rows, :] = (vhat * par["gate_gain"][...] + par["gate_bias"][...]).astype(BF16)
    last = lax.broadcasted_iota(jnp.int32, (16, 1), 0) == 15
    gate[rows - 16 : rows, :] = jnp.where(last, 1.0, gate[rows - 16 : rows, :].astype(F32)).astype(BF16)
    scr["hs"][0:rows, :] = jnp.zeros((rows, 128), F32)
    scr["hv"][0:rows, :] = jnp.zeros((rows, 128), F32)

    @pl.loop(0, tiles, unroll=tiles)
    def _(t):
        at = pl.ds(pl.multiple_of(t * CT, CT), CT)
        z = dot(act[0:rows, :], par["w_in"][:, at]) + par["b_in"][:, at]
        u, slope = gelu_both(z)
        sp = dot(par["wsp"][kind], gate[0:rows, at]) + par["bsp"][kind, :, 0:1]
        gated[0:rows, at] = (u * sp).astype(BF16)
        dg = dot_nt(dbr[0:rows, :], par["w_out"][at, :])
        pre = (dg * sp * slope).astype(BF16)
        dpre[0:rows, at] = pre
        ds = (dg * u).astype(BF16)
        dsp[0:rows, at] = ds
        dgate = dot(par["wsp_t"][kind], ds)
        vh = vs[0:rows, at]
        acc["gate_bias"][:, at] += col8(dgate)
        acc["gate_gain"][:, at] += col8(dgate * vh)
        h = dgate * par["gate_gain"][:, at]
        dgs[0:rows, at] = h
        scr["hs"][0:rows, :] += fold(h)
        scr["hv"][0:rows, :] += fold(h * vh)

    hmean = jnp.sum(scr["hs"][0:rows, :], axis=-1, keepdims=True) / half
    hvmean = jnp.sum(scr["hv"][0:rows, :], axis=-1, keepdims=True) / half

    @pl.loop(0, tiles, unroll=tiles)
    def _(t):
        at = pl.ds(pl.multiple_of(t * CT, CT), CT)
        far = pl.ds(pl.multiple_of(half + t * CT, CT), CT)
        dv = vinv * (dgs[0:rows, at] - hmean - vs[0:rows, at] * hvmean)
        pre = (dv * gvp[0:rows, at].astype(F32)).astype(BF16)
        dpre[0:rows, far] = pre

    mixed = dot_nt(dsp[0:rows, :], gate[0:rows, :])
    for c in range(acc["w_sp"].shape[0]):
        acc["w_sp"][c, :, 0:rows] += jnp.where(kind == c + 1, mixed, 0.0)
    branch = dot(gated[0:rows, :], par["w_out"][...]) + par["b_out"][...]
    dys[0:rows, :] = branch * KEEP
    dact = dot_nt(dpre[0:rows, :], par["w_in"][...])
    xhat = xs[0:rows, :]
    acc["ln_bias"][...] += col8(dact)
    acc["ln_gain"][...] += col8(dact * xhat)
    h = dact * par["ln_gain"][...]
    back = scr["inv"][0:rows, 0:1] * (
        h - jnp.mean(h, axis=-1, keepdims=True) - xhat * jnp.mean(h * xhat, axis=-1, keepdims=True)
    )
    xs[0:rows, :] = back
    for m in range(groups):

        @pl.when(me == m)
        def _(m=m):
            for k in range(groups):
                at = (m ^ k) * slot_count
                stage[0:slot_count, :] = dys[at : at + slot_count, :]
                stage[slot_count : 2 * slot_count, :] = xs[at : at + slot_count, :]
                parcel[k, slot] = stage[...].astype(BF16)


VECTORS = ("b_in", "gate_gain", "gate_bias", "ln_gain", "ln_bias", "b_out", "b_sp")
LARGE = ("w_in", "w_out")
TABLES = ("wsp", "wsp_t", "bsp", "live", "pick")
ACC = ("w_sp", "gate_gain", "gate_bias", "ln_gain", "ln_bias", "b_out", "w_in", "w_out")
SCR = ("stage", "xs", "dys", "inv", "vs", "gvp", "gate", "dsp", "dgs", "hs", "hv")
KEPT = ("act", "dbr", "gated", "dpre")


def reduce_orders(dp):
    bits = [1 << b for b in range(dp.bit_length() - 1)]
    x, z, y = [("dp", bits[:1])], [("dp", [bit]) for bit in bits[1:3]], [("patch", [2])]
    rest = [("dp", [bit]) for bit in bits[3:]]
    return {
        "a": x + y + z + rest, "b": y + x + z + rest, "c": z + x + y + rest, "d": x + z + y + rest, "e": y + z + x + rest,
    }


def combos(bits):
    masks = [0]
    for bit in bits:
        masks += [mask | bit for mask in masks]
    return masks[1:]


def plan_sizes(order, rows):
    sizes = [rows]
    for _, bits in order:
        keep = sizes[-1] >> len(bits)
        sizes.append(keep if keep >= 16 else sizes[-1])
    return sizes


LINES = ("gate_gain", "gate_bias", "ln_gain", "ln_bias", "b_out")


def fill_tables(par, quarter, slot_count, groups):
    side = par["wsp"].shape[1]
    t = lax.broadcasted_iota(jnp.int32, (side, 1), 0)
    lane = lax.broadcasted_iota(jnp.int32, (1, slot_count * groups), 1)
    lanes = lax.broadcasted_iota(jnp.int32, (1, side), 1)
    place = sum(jnp.where(t >= slot_count * g, 1, 0) for g in range(1, groups))
    within = t - slot_count * place
    w = par["w_sp"][...]
    for name in ("wsp", "wsp_t", "bsp", "live"):
        par[name][0] = jnp.zeros(par[name].shape[1:], par[name].dtype)
    for c, q in enumerate(quarter):
        live = (within < q) & (t < slot_count * groups)
        hit = live & (place * q + within == lane)
        low = jnp.where(hit, 1.0, 0.0).astype(BF16)
        par["wsp"][c + 1] = dot_nt(dot(low, w).astype(BF16), low).astype(BF16)
        par["wsp_t"][c + 1] = dot_nt(dot_nt(low, w).astype(BF16), low).astype(BF16)
        bias = jnp.sum(jnp.where(hit, par["b_sp"][...], 0.0), axis=-1, keepdims=True)
        par["bsp"][c + 1] = jnp.broadcast_to(bias, (side, 128))
        par["live"][c + 1] = jnp.broadcast_to(jnp.where(live, KEEP, 0.0), (side, 128))
        if c < 2:
            corner = (t == side - 1) & (lanes == side - 1)
            chosen = (live & (place * q + within == lanes)) | corner
            par["pick"][c] = jnp.where(chosen, 1.0, 0.0).astype(BF16)


def gather_gradients(total_ref, par, acc, kept):
    act_t = jnp.concatenate([kept["act"][...].T, jnp.ones((16, kept["act"].shape[0]), BF16)], axis=0)
    for t in range(acc["w_in"].shape[1] // CT):
        at = slice(t * CT, (t + 1) * CT)
        acc["w_in"][:, at] += dot(act_t, kept["dpre"][:, at])
    dbr_t = kept["dbr"][...].T
    for t in range(acc["w_out"].shape[1] // CT):
        at = slice(t * CT, (t + 1) * CT)
        acc["w_out"][:, at] += dot(dbr_t, kept["gated"][:, at])


def lay_out(total_ref, par, acc):
    width, half = acc["w_out"].shape
    wide = acc["w_in"].shape[1]
    base = wide + half
    rows, span = acc["w_sp"].shape[1:]
    total_ref[:, 0:wide] = acc["w_in"][0:width, :].astype(BF16)
    total_ref[:, wide:base] = acc["w_out"][...].astype(BF16)
    mix = acc["w_sp"][2, :, 0:rows]
    for c in range(2):
        pick = par["pick"][c]
        part = dot(acc["w_sp"][c, :, 0:rows].astype(BF16), pick).astype(BF16)
        mix = mix + dot_tn(pick, part)
    total_ref[:, base:] = jnp.zeros((width, total_ref.shape[1] - base), BF16)
    total_ref[0:rows, base : base + rows] = mix.astype(BF16)
    lines = []
    for name in LINES:
        v = jnp.sum(acc[name][...], axis=0, keepdims=True)
        lines += [v[:, i * width : (i + 1) * width] for i in range(v.shape[1] // width)]
    more = [acc["w_in"][width : width + 1, i * width : (i + 1) * width] for i in range(wide // width)]
    more.append(jnp.zeros((32 - len(lines) - len(more), width), F32))
    total_ref[rows : rows + 32, base : base + width] = jnp.concatenate(lines + more, axis=0).astype(BF16)


def layer_kernel(orders, spans, sizes, slot_count, groups, quarter, pair, cls_ref, *refs):
    depth = len(orders[0])
    packed, refs = refs[:groups], refs[groups:]
    weights, w_sp_ref, given, refs = refs[:2], refs[2], refs[3 : 3 + len(VECTORS)], refs[3 + len(VECTORS) :]
    out_ref, back_ref, total_ref, parcel, *refs = refs
    names = TABLES + LARGE + VECTORS
    par, refs = {"w_sp": w_sp_ref} | dict(zip(names, refs)), refs[len(names) :]
    acc, refs = dict(zip(ACC, refs)), refs[len(ACC) :]
    scr, refs = dict(zip(SCR, refs)), refs[len(SCR) :]
    kept, refs = dict(zip(KEPT, refs)), refs[len(KEPT) :]
    first, *refs = refs
    rbufs, refs = refs[:depth], refs[depth:]
    send_sem, recv_sem, in_send, in_recv, back_send, back_recv, own_sem, load_sem = refs
    dp, patch = lax.axis_index("dp"), lax.axis_index("patch")
    core = patch & 1

    def peer(axis, bit):
        return (dp ^ bit, patch) if axis == "dp" else (dp, patch ^ bit)

    peers = [peer("patch", 1), peer("patch", 3)] + [peer(a, mask) for a, bits in orders[0] for mask in combos(bits)]
    barrier = pltpu.get_barrier_semaphore()
    for other in peers:
        pl.semaphore_signal(barrier, inc=1, device_id=other, device_id_type=MESH)
    pl.semaphore_wait(barrier, len(peers))

    slots = parcel.shape[1]

    def inward(k, j):
        if k == 0:
            return pltpu.make_async_copy(packed[0].at[j], parcel.at[0, j], own_sem.at[0, j])
        return pltpu.make_async_remote_copy(
            src_ref=packed[k].at[j], dst_ref=parcel.at[k, j], send_sem=in_send.at[k, j], recv_sem=in_recv.at[k, j],
            device_id=peer("patch", k), device_id_type=MESH,
        )

    def back(k, j):
        place = j * groups + jnp.where(lax.rem(j, 2) == 0, patch, groups - 1 - patch)
        if k == 0:
            return pltpu.make_async_copy(parcel.at[0, j], back_ref.at[place], own_sem.at[1, j])
        return pltpu.make_async_remote_copy(
            src_ref=parcel.at[k, j], dst_ref=back_ref.at[place], send_sem=back_send.at[k, j], recv_sem=back_recv.at[k, j],
            device_id=peer("patch", k), device_id_type=MESH,
        )

    def give_back(begin, end):
        @pl.loop(begin, end)
        def _(j):
            for k in range(groups - 1, -1, -1):
                back(k, j).start()

    stops = [slots * n // 6 for n in (0, *BACKS, 6)]

    @pl.loop(0, slots)
    def _(j):
        for k in range(groups - 1, -1, -1):
            inward(k, j).start()

    loads = [pltpu.make_async_copy(weights[i], par[name], load_sem.at[i]) for i, name in enumerate(LARGE)]
    for load in loads:
        load.start()
    for name, ref in zip(VECTORS, given):
        par[name][...] = ref[...].reshape(1, ref.shape[0])
    fill_tables(par, quarter, slot_count, groups)
    for ref in acc.values():
        ref[...] = jnp.zeros_like(ref)
    rows = scr["xs"].shape[0]
    for ref in kept.values():
        if ref.shape[0] > pair * rows:
            ref[pair * rows :, :] = jnp.zeros((ref.shape[0] - pair * rows, ref.shape[1]), BF16)
    n = groups * slot_count
    for name in ("xs", "dys"):
        scr[name][rows - 16 : rows, :] = jnp.zeros((16, scr[name].shape[1]), F32)
    for load in loads:
        load.wait()

    @pl.loop(0, slots)
    def _(j):
        for k in range(groups):
            inward(k, j).wait()

        @pl.when(j == slots - 2)
        def _():
            give_back(stops[0], stops[1])

        @pl.when(j == slots - 1)
        def _():
            give_back(stops[1], stops[2])

        half_at = pl.ds(pl.multiple_of(lax.rem(j, pair) * rows, 16), rows)
        views = {name: ref.at[half_at] for name, ref in kept.items()}
        image_work(cls_ref[j], j, slot_count, patch, parcel, par, acc, scr | views)

        @pl.when(lax.rem(j, pair) == pair - 1)
        def _():
            gather_gradients(total_ref, par, acc, kept)

    lay_out(total_ref, par, acc)
    half = total_ref.shape[1] // 2
    tall = total_ref.shape[0]
    pieces = len(orders)
    mine = pl.multiple_of(core * half, 128)
    theirs = pl.multiple_of((1 - core) * half, 128)
    copies = []

    def send(src, dst, step, i, part, other):
        copy = pltpu.make_async_remote_copy(
            src_ref=src, dst_ref=dst, send_sem=send_sem.at[part, step, i], recv_sem=recv_sem.at[part, step, i], device_id=other,
            device_id_type=MESH,
        )
        copy.start()
        copies.append(copy)
        return copy

    def cols(i):
        return pl.ds(spans[i][0], spans[i][1])

    def shifted(base, i):
        return pl.ds(pl.multiple_of(base + spans[i][0], 128), spans[i][1])

    def rank_in(axis, bits):
        index = dp if axis == "dp" else patch
        return sum(jnp.where((index & bit) != 0, 1 << n, 0) for n, bit in enumerate(bits))

    def other_rank(axis, bits, mask):
        index = (dp if axis == "dp" else patch) ^ mask
        return sum(jnp.where((index & bit) != 0, 1 << n, 0) for n, bit in enumerate(bits))

    def rows_at(begin, size):
        return pl.ds(pl.multiple_of(begin, 16), size)

    state = [0] * pieces
    flying = [
        [send(total_ref.at[:, shifted(theirs, i)], first.at[:, cols(i)], 0, i, 0, peer("patch", 1))] for i in range(pieces)
    ]
    give_back(stops[2], stops[3])
    for s in range(depth + 1):
        if s == 2:
            give_back(stops[3], stops[4])
        for i in range(pieces):
            size = sizes[i][s]
            for copy in flying[i]:
                copy.wait_recv()
            lo = state[i]
            if s > 0 and sizes[i][s - 1] == size:
                for copy in flying[i]:
                    copy.wait_send()
                copies[:] = [copy for copy in copies if all(copy is not old for old in flying[i])]
            got_ref = first if s == 0 else rbufs[s - 1]
            unit = 32 if size % 32 == 0 else 16

            @pl.loop(0, size, step=unit)
            def _(r, i=i, lo=lo, got_ref=got_ref, unit=unit, size=size, parts=len(flying[i])):
                at = rows_at(lo + r, unit)
                value = total_ref[at, shifted(mine, i)].astype(F32)
                for part in range(parts):
                    value = value + got_ref[rows_at(part * size + r, unit), cols(i)].astype(F32)
                total_ref[at, shifted(mine, i)] = value.astype(BF16)

            if s < depth:
                axis, bits = orders[i][s]
                keep = sizes[i][s + 1]
                base = state[i]
                split = keep < size
                if split:
                    state[i] = base + rank_in(axis, bits) * keep
                flying[i] = []
                for part, mask in enumerate(combos(bits)):
                    give = base + other_rank(axis, bits, mask) * keep if split else base
                    flying[i].append(
                        send(
                            total_ref.at[rows_at(give, keep), shifted(mine, i)],
                            rbufs[s].at[pl.ds(part * keep, keep), cols(i)], s + 1, i, part, peer(axis, mask),
                        )
                    )
    for i in range(pieces):
        at = rows_at(state[i], sizes[i][depth])
        out_ref[at, shifted(mine, i)] = total_ref[at, shifted(mine, i)]
    flying = [[] for _ in range(pieces)]
    for s in range(depth, -1, -1):
        if s == depth - 1:
            give_back(stops[4], stops[5])
        for i in range(pieces):
            for copy in flying[i]:
                copy.wait_recv()
            flying[i] = []
            step = 2 * depth + 1 - s
            if s == 0:
                where = out_ref.at[:, shifted(mine, i)]
                flying[i] = [send(where, where, step, i, 0, peer("patch", 1))]
            elif sizes[i][s] < sizes[i][s - 1]:
                axis, bits = orders[i][s - 1]
                where = out_ref.at[rows_at(state[i], sizes[i][s]), shifted(mine, i)]
                for part, mask in enumerate(combos(bits)):
                    flying[i].append(send(where, where, step, i, part, peer(axis, mask)))
                state[i] = state[i] - rank_in(axis, bits) * sizes[i][s]
    for i in range(pieces):
        for copy in flying[i]:
            copy.wait_recv()

    @pl.loop(0, slots)
    def _(j):
        for k in range(groups):
            back(k, j).wait()

    for copy in copies:
        copy.wait_send()


def call_layer(cls, packed, w_in, w_out, w_spatial, vectors, dp, groups, slot_count, quarter, pieces):
    slots, stage_rows, width = packed[0].shape
    wide, half, side = w_in.shape[1], w_out.shape[0], up(w_spatial.shape[0], 16)
    span = up(side, 128)
    pair = PAIR if slots % PAIR == 0 else 1
    columns = wide + half + width
    table = reduce_orders(dp)
    orders = [table[name] for name, _ in pieces]
    starts = np.cumsum([0] + [w * 128 for _, w in pieces])
    spans = [(int(starts[i]), w * 128) for i, (_, w) in enumerate(pieces)]
    depth = len(orders[0])
    sizes = [plan_sizes(order, width) for order in orders]
    room_for = [
        max(len(combos(order[s][1])) * size[s + 1] for order, size in zip(orders, sizes)) for s in range(depth)
    ]
    fan = max(len(combos(bits)) for _, bits in orders[0])
    vmem = pl.BlockSpec(memory_space=pltpu.VMEM)
    far = pl.BlockSpec(memory_space=pl.ANY)
    acc = {
        "w_sp": (3, side, span), "gate_gain": (8, half), "gate_bias": (8, half), "ln_gain": (8, width),
        "ln_bias": (8, width), "b_out": (8, width), "w_in": (width + 16, wide), "w_out": (width, half),
    }
    scr = {
        "stage": ((stage_rows, width), F32), "xs": ((side, width), F32), "dys": ((side, width), F32),
        "inv": ((side, 128), F32), "vs": ((side, half), F32), "gvp": ((side, half), BF16), "gate": ((side, half), BF16),
        "dsp": ((side, half), BF16), "dgs": ((side, half), F32), "hs": ((side, 128), F32), "hv": ((side, 128), F32),
    }
    room = up(pair * side, 256)
    return pl.pallas_call(
        functools.partial(layer_kernel, orders, spans, sizes, slot_count, groups, quarter, pair),
        out_shape=[
            jax.ShapeDtypeStruct((width, columns), BF16),
            jax.ShapeDtypeStruct((slots * groups, stage_rows, width), BF16),
        ],
        in_specs=[pl.BlockSpec(memory_space=pltpu.SMEM)] + [far] * groups + [far, far, vmem] + [vmem] * len(vectors),
        out_specs=[vmem, far],
        scratch_shapes=[pltpu.VMEM((width, columns), BF16), pltpu.VMEM((groups, slots, stage_rows, width), BF16)]
        + [pltpu.VMEM((n, side, m), t) for n, m, t in ((4, side, BF16), (4, side, BF16), (4, 128, F32), (4, 128, F32), (2, side, BF16))]
        + [pltpu.VMEM(w_in.shape, BF16), pltpu.VMEM(w_out.shape, BF16)]
        + [pltpu.VMEM((1, v.shape[0]), F32) for v in vectors]
        + [pltpu.VMEM(acc[name], F32) for name in ACC]
        + [pltpu.VMEM(*scr[name]) for name in SCR]
        + [pltpu.VMEM((room, n), BF16) for n in (width, width, half, wide)]
        + [pltpu.VMEM((width, columns // 2), BF16)]
        + [pltpu.VMEM((size, columns // 2), BF16) for size in room_for]
        + [pltpu.SemaphoreType.DMA((fan, 2 * depth + 2, len(pieces)))] * 2
        + [pltpu.SemaphoreType.DMA((groups, slots))] * 4
        + [pltpu.SemaphoreType.DMA((2, slots)), pltpu.SemaphoreType.DMA((2,))],
        compiler_params=pltpu.CompilerParams(
            collective_id=1, has_side_effects=True, vmem_limit_bytes=64 * 1024 * 1024 - 65536
        ),
        name="layer",
    )(cls, *packed, w_in, w_out, w_spatial, *vectors)


def local(images, cotangent, res_class, skip, ln_gain, ln_bias, w_in, b_in, gate_gain, gate_bias, w_spatial, b_spatial, w_out, b_out):
    groups = lax.axis_size("patch")
    dp = lax.axis_size("dp")
    count, slot_count, width = images.shape
    half = w_out.shape[0]
    wide = w_in.shape[1]
    slots = count // groups
    quarter = tuple(side * side // groups for side in SIDES)
    patches = groups * slot_count
    side = up(patches, 16)
    stage_rows = up(2 * slot_count, 16)
    me = lax.axis_index("patch").astype(jnp.int32)

    key = jnp.where(skip != 0, res_class + 1, 0).astype(jnp.int32)
    index = jnp.arange(count, dtype=jnp.int32)
    before = (key[None, :] > key[:, None]) | ((key[None, :] == key[:, None]) & (index[None, :] < index[:, None]))
    rank = jnp.sum(before.astype(jnp.int32), axis=1)
    hit = rank[None, :] == index[:, None]
    order = jnp.sum(jnp.where(hit, index[None, :], 0), axis=1)
    slot_index = jnp.arange(slots, dtype=jnp.int32)
    spot = slot_index * groups + jnp.where(slot_index % 2 == 0, me, groups - 1 - me)
    cls = jnp.sum(jnp.where(spot[:, None] == rank[None, :], key[None, :], 0), axis=1)
    me1 = me.reshape(1)

    whole = pl.BlockSpec(memory_space=pltpu.VMEM)
    smem = pl.BlockSpec(memory_space=pltpu.SMEM)
    img_t = jnp.swapaxes(images, 0, 1)
    cot_t = jnp.swapaxes(cotangent, 0, 1)
    planes = (width // 128, (up(slot_count, 8) + 1) * count, 128)
    packed = pl.pallas_call(
        functools.partial(pack_kernel, slot_count, groups),
        out_shape=[jax.ShapeDtypeStruct((slots, stage_rows, width), BF16)] * groups,
        in_specs=[smem, smem, whole, whole],
        out_specs=[pl.BlockSpec(memory_space=pltpu.HBM)] * groups,
        scratch_shapes=[pltpu.VMEM((groups, slots, stage_rows, width), BF16), pltpu.VMEM(planes, F32), pltpu.VMEM(planes, F32)]
        + [pltpu.VMEM((stage_rows, width), F32), pltpu.SemaphoreType.DMA((groups, slots))],
        compiler_params=pltpu.CompilerParams(vmem_limit_bytes=62 * 1024 * 1024),
        name="pack",
    )(me1, order, img_t, cot_t)

    vectors = (b_in, gate_gain, gate_bias, ln_gain, ln_bias, b_out, b_spatial)
    summed, backs = call_layer(cls, packed, w_in, w_out, w_spatial, vectors, dp, groups, slot_count, quarter, PIECES)
    cut = 512
    inner, outer = wide // cut, half // cut
    far = pl.BlockSpec(memory_space=pl.ANY)
    rowed = [jax.ShapeDtypeStruct((n,), F32) for n in (half, half, width, width, width, wide)]
    swapped = (slot_count, count, width)
    results = pl.pallas_call(
        functools.partial(finish_kernel, slot_count, quarter, wide, half),
        out_shape=[
            jax.ShapeDtypeStruct((width, wide), F32), jax.ShapeDtypeStruct((half, width), F32),
            jax.ShapeDtypeStruct((patches, patches), F32), jax.ShapeDtypeStruct((patches,), F32),
            *rowed, jax.ShapeDtypeStruct(swapped, BF16), jax.ShapeDtypeStruct(swapped, F32),
        ],
        grid=(1 + inner + outer,),
        in_specs=[smem, smem, far, far, far]
        + [pl.BlockSpec((width, cut), lambda t: (0, jnp.where(t == 0, inner + outer, t - 1)))],
        out_specs=[
            pl.BlockSpec((width, cut), lambda t: (0, jnp.clip(t - 1, 0, inner - 1))),
            pl.BlockSpec((cut, width), lambda t: (jnp.maximum(t - 1 - inner, 0), 0)),
        ]
        + [whole] * 8
        + [far, far],
        scratch_shapes=[pltpu.VMEM(planes, F32), pltpu.VMEM(planes, F32), pltpu.VMEM((stage_rows, width), F32)]
        + [pltpu.VMEM(swapped, BF16), pltpu.VMEM(swapped, F32), pltpu.VMEM(swapped, BF16), pltpu.VMEM(swapped, BF16)]
        + [pltpu.VMEM(backs.shape, BF16), pltpu.SemaphoreType.DMA((5,))],
        compiler_params=pltpu.CompilerParams(vmem_limit_bytes=56 * 1024 * 1024),
        name="finish",
    )(rank, key, img_t, cot_t, backs, summed)
    g_w_in, g_w_out, g_w_sp, g_b_sp, g_gate_gain, g_gate_bias, g_ln_gain, g_ln_bias, g_b_out, g_b_in, out_t, grad_t = results
    return (
        jnp.swapaxes(out_t, 0, 1), jnp.swapaxes(grad_t, 0, 1), g_ln_gain, g_ln_bias, g_w_in, g_b_in,
        g_gate_gain, g_gate_bias, g_w_sp, g_b_sp, g_w_out, g_b_out,
    )


def solution(mesh):
    placed = (P("dp", "patch", None),) * 2 + (P("dp"),) * 2 + (P(),) * 10
    return jax.shard_map(
        local, mesh=mesh, in_specs=placed, out_specs=(P("dp", "patch", None),) * 2 + (P(),) * 10, check_vma=False,
    )
```
